512 devices in a mesh: seq: 64 (over x, z), head: 8 (over y, core).
Axes of the slice: x: 4, y: 4, z: 16, core: 2. Of those that a mesh axis runs over, the one named last changes fastest.
Arguments:
- lat_query: bfloat16 [256, 1024], P(None, 'head'), may hold values from -20 to 20
- pkt_key: bfloat16 [147456, 1024], P('seq', 'head'), may hold values from -20 to 20
- pkt_value: bfloat16 [147456, 1024], P('seq', 'head'), may hold values from -6 to 6
- enc_grad: bfloat16 [256, 1024], P(None, 'head'), may hold values from -6 to 6
- pkt_query: bfloat16 [147456, 1024], P('seq', 'head'), may hold values from -20 to 20
- lat_key: bfloat16 [256, 1024], P(None, 'head'), may hold values from -20 to 20
- lat_value: bfloat16 [256, 1024], P(None, 'head'), may hold values from -6 to 6
- dec_grad: bfloat16 [147456, 1024], P('seq', 'head'), may hold values from -6 to 6
- row_mask: int32 [147456], P(('seq', 'head')), may hold values 0 or 1
Outputs:
- grad_lat_query: bfloat16 [256, 1024], P(None, 'head')
- grad_pkt_key: bfloat16 [147456, 1024], P('seq', 'head')
- grad_pkt_value: bfloat16 [147456, 1024], P('seq', 'head')
- grad_pkt_query: bfloat16 [147456, 1024], P('seq', 'head')
- grad_lat_key: bfloat16 [256, 1024], P(None, 'head')
- grad_lat_value: float32 [256, 1024], P(None, 'head')
The draws below stay inside these ranges and needn't reach their ends.
All inputs are finite; a program needn't handle non-finite values. No bound on the sum of `row_mask` on one device may be relied on, other than what follows from the above.
Results may differ from the reference program's by a relative error of at most 0.023.
Values sent between devices are 32-bit elements; how exact they have to be, the bound alone decides.
A program may use at most 64 MiB of HBM per device.

```python
import math
import jax
import jax.numpy as jnp
from jax import lax

LATENTS = 256
HEADS = 8
DH = 128
WIDTH = 1024
PACKETS = 147456


def base_rows(key, count):
    return jnp.clip(jax.random.normal(key, (count, HEADS * DH), jnp.float32), -4.0, 4.0)


def draw_lat_query(key, part):
    key = jax.random.fold_in(key, 11)
    base = 2.0 * base_rows(key, LATENTS)
    return base.astype(jnp.bfloat16)


def draw_pkt_key(key, part):
    key = jax.random.fold_in(key, 12)
    base = base_rows(key, PACKETS)
    return base.astype(jnp.bfloat16)


def draw_pkt_query(key, part):
    key = jax.random.fold_in(key, 13)
    base = base_rows(key, PACKETS)
    return base.astype(jnp.bfloat16)


def draw_lat_key(key, part):
    key = jax.random.fold_in(key, 14)
    base = base_rows(key, LATENTS)
    return base.astype(jnp.bfloat16)


def touch_ends(array, own_key, least, top_value):
    spot = [jax.random.randint(jax.random.fold_in(own_key, axis), (), 0, length) for axis, length in enumerate(array.shape)]
    main_axis = array.shape.index(max(array.shape))
    next_to = spot[:main_axis] + [(spot[main_axis] + 1) % array.shape[main_axis]] + spot[main_axis + 1:]
    return array.at[tuple(spot)].set(least).at[tuple(next_to)].set(top_value)


def block_levels(rng, extent, pieces, least, top_value):
    loudness, own = 1.0, jax.random.fold_in(rng, 6)
    for axis_at, blocks in pieces:
        steps = jnp.exp(jax.random.uniform(jax.random.fold_in(own, axis_at), (blocks,), jnp.float32, least / len(pieces), top_value / len(pieces)))
        loudness = loudness * jnp.repeat(steps, extent[axis_at] // blocks).reshape([-1 if axis == axis_at else 1 for axis in range(len(extent))])
    return loudness


def gaussian(rng, dims, scale, reach, split=(), kind=jnp.bfloat16):
    result = jax.random.normal(rng, dims, jnp.float32) * scale
    if len(split) > 0:
        result = block_levels(rng, dims, split, -0.22, 0.18) * result
    return jnp.clip(result, min=-reach, max=reach).astype(kind)


def setup_inputs(seed: int = 0) -> dict:
    key_of = jax.random.split(jax.random.key(seed), 10)
    lat_query = draw_lat_query(jax.random.fold_in(key_of[9], 71), 0)
    pkt_key = draw_pkt_key(jax.random.fold_in(key_of[9], 71), 0)
    pkt_value = gaussian(key_of[2], (PACKETS, WIDTH), 1.0, 6.0, ((0, 64), (1, 8)))
    enc_grad = gaussian(key_of[3], (LATENTS, WIDTH), 1.0, 6.0, ((1, 8),))
    pkt_query = draw_pkt_query(jax.random.fold_in(key_of[9], 71), 0)
    lat_key = draw_lat_key(jax.random.fold_in(key_of[9], 71), 0)
    lat_value = gaussian(key_of[6], (LATENTS, WIDTH), 1.0, 6.0, ((1, 8),))
    dec_grad = gaussian(key_of[7], (PACKETS, WIDTH), 1.0, 6.0, ((0, 64), (1, 8)))
    row_mask = touch_ends((jax.random.randint(key_of[8], (PACKETS,), 0, 8) < 7).astype(jnp.int32), jax.random.fold_in(key_of[8], 1), 0, 1)
    return dict(lat_query=lat_query, pkt_key=pkt_key, pkt_value=pkt_value, enc_grad=enc_grad, pkt_query=pkt_query, lat_key=lat_key, lat_value=lat_value, dec_grad=dec_grad, row_mask=row_mask)


def by_head(x):
    return x.reshape(x.shape[0], HEADS, DH).transpose(1, 0, 2)

def join_heads(x):
    return x.transpose(1, 0, 2).reshape(x.shape[1], HEADS * DH)

def encoder_head(query, keys, values, grad_out, valid):
    scale = 1.0 / math.sqrt(DH)
    scores = jnp.dot(query, keys.T, preferred_element_type=jnp.float32) * scale
    scores = jnp.where(valid[None, :], scores, -1e+30)
    top = lax.optimization_barrier(jnp.max(scores, axis=1, keepdims=True))
    expo = jnp.where(valid[None, :], jnp.exp(scores - top), 0.0)
    probs = expo / lax.optimization_barrier(jnp.sum(expo, axis=1, keepdims=True))
    dprob = jnp.dot(grad_out, values.T, preferred_element_type=jnp.float32)
    delta = lax.optimization_barrier(jnp.sum(probs * dprob, axis=1, keepdims=True))
    dscore = (probs * (dprob - delta)).astype(jnp.bfloat16)
    grad_query = (jnp.dot(dscore, keys, preferred_element_type=jnp.float32) * scale).astype(jnp.bfloat16)
    grad_keys = (jnp.dot(dscore.T, query, preferred_element_type=jnp.float32) * scale).astype(jnp.bfloat16)
    grad_values = jnp.dot(probs.astype(jnp.bfloat16).T, grad_out, preferred_element_type=jnp.float32).astype(jnp.bfloat16)
    return (grad_query, grad_keys, grad_values)

def decoder_head(query, keys, values, grad_out, valid):
    scale = 1.0 / math.sqrt(DH)
    scores = jnp.dot(query, keys.T, preferred_element_type=jnp.float32) * scale
    top = lax.optimization_barrier(jnp.max(scores, axis=1, keepdims=True))
    expo = jnp.exp(scores - top)
    probs = expo / lax.optimization_barrier(jnp.sum(expo, axis=1, keepdims=True))
    masked = jnp.where(valid[:, None], grad_out, jnp.zeros_like(grad_out))
    dprob = jnp.dot(masked, values.T, preferred_element_type=jnp.float32)
    delta = lax.optimization_barrier(jnp.sum(probs * dprob, axis=1, keepdims=True))
    dscore = (probs * (dprob - delta)).astype(jnp.bfloat16)
    grad_query = (jnp.dot(dscore, keys, preferred_element_type=jnp.float32) * scale).astype(jnp.bfloat16)
    grad_keys = (jnp.dot(dscore.T, query, preferred_element_type=jnp.float32) * scale).astype(jnp.bfloat16)
    grad_values = jnp.dot(probs.astype(jnp.bfloat16).T, masked, preferred_element_type=jnp.float32)
    return (grad_query, grad_keys, grad_values)

def reference(lat_query, pkt_key, pkt_value, enc_grad, pkt_query, lat_key, lat_value, dec_grad, row_mask):
    valid = row_mask > 0
    encoded = lax.map(lambda group: encoder_head(group[0], group[1], group[2], group[3], valid), (by_head(lat_query), by_head(pkt_key), by_head(pkt_value), by_head(enc_grad)))
    decoded = lax.map(lambda group: decoder_head(group[0], group[1], group[2], group[3], valid), (by_head(pkt_query), by_head(lat_key), by_head(lat_value), by_head(dec_grad)))
    return (join_heads(encoded[0]), join_heads(encoded[1]), join_heads(encoded[2]), join_heads(decoded[0]), join_heads(decoded[1]), join_heads(decoded[2]))
```

```python
import functools
import math

import jax
import jax.numpy as jnp
from jax import lax
from jax.experimental import pallas as pl
from jax.experimental.pallas import tpu as pltpu
from jax.sharding import PartitionSpec as P

DH = 128
LAT = 256
NZ = 16
MESH = pl.DeviceIdType.MESH
F32 = jnp.float32
BF16 = jnp.bfloat16
NT = (((1,), (1,)), ((), ()))
NN = (((1,), (0,)), ((), ()))
TN = (((0,), (0,)), ((), ()))


def dot(a, b, dims):
    return lax.dot_general(a, b, dims, preferred_element_type=F32)


def merge_stats(ref, count):
    lses = [ref[i, 0:2, :] for i in range(count)]
    top = functools.reduce(jnp.maximum, lses)
    weights = [jnp.exp(lse - top) for lse in lses]
    total = functools.reduce(jnp.add, weights)
    mixed = functools.reduce(jnp.add, [w * ref[i, 2:4, :] for i, w in enumerate(weights)])
    return top + jnp.log(total), mixed / total


def fold(line):
    return jnp.concatenate([line[:, :128], line[:, 128:]], axis=0)


def kernel(
    nx, nh, rows,
    lq_hbm, pk_hbm, pv_hbm, eg_hbm, pq_hbm, lk_hbm, lv_hbm, dg_hbm, mask_hbm,
    glq_ref, gpk_ref, gpv_ref, gpq_ref, glk_ref, glv_ref,
    lq_ref, pk_ref, pv_ref, eg_ref, pq_ref, lk_ref, lv_ref, dg_ref, mask_ref,
    maskbuf, mcol, expo, edot, chunk_top, dprob, query_t,
    sx, sz, pdec, rxdec, sumdec, rzdec, fulldec, pq, rxq, sumq, rzq, fullq,
    in_sems,
    m_send, m_recv, sx_send, sx_recv, sz_send, sz_recv,
    dx_send, dx_recv, dz_send, dz_recv, daz_send, daz_recv, dax_send, dax_recv,
    qx_send, qx_recv, qz_send, qz_recv, qaz_send, qaz_recv, qax_send, qax_recv,
):
    scale = 1.0 / math.sqrt(DH)
    piece = rows // nh
    chunks = 4
    size = rows // chunks
    seq = lax.axis_index("seq")
    head = lax.axis_index("head")
    xi = seq // NZ
    zi = lax.rem(seq, NZ)

    loads = [
        pltpu.make_async_copy(src, dst, in_sems.at[i])
        for i, (src, dst) in enumerate(
            (
                (mask_hbm, mask_ref),
                (pq_hbm, pq_ref),
                (lk_hbm, lk_ref),
                (dg_hbm, dg_ref),
                (lv_hbm, lv_ref),
                (pk_hbm, pk_ref),
                (lq_hbm, lq_ref),
                (pv_hbm, pv_ref),
                (eg_hbm, eg_ref),
            )
        )
    ]
    for load in loads:
        load.start()

    def head_peer(step):
        return lax.rem(head + step, nh)

    def x_peer(step):
        return lax.rem(xi + step, nx)

    def z_peer(step):
        return lax.rem(zi + NZ // 2 + (step // 2) * (2 * lax.rem(step, 2) - 1), NZ)

    def at_head(peer):
        return (seq, peer)

    def at_x(peer):
        return (peer * NZ + zi, head)

    def at_z(peer):
        return (xi * NZ + peer, head)

    def every(count, body):
        def step(i, carry):
            body(i)
            return carry

        lax.fori_loop(1, count, step, 0)

    def send(src, dst, send_sem, recv_sem, target):
        return pltpu.make_async_remote_copy(
            src_ref=src, dst_ref=dst, send_sem=send_sem.at[0], recv_sem=recv_sem.at[0],
            device_id=target, device_id_type=MESH,
        )

    def all_of(ref, count, send_sem, recv_sem, target):
        part = ref.at[pl.ds(0, count - 1)]
        return send(part, part, send_sem, recv_sem, target)

    barrier = pltpu.get_barrier_semaphore()

    def greet(peer_of, place):
        def body(step):
            pl.semaphore_signal(
                barrier, inc=1, device_id=place(peer_of(step)), device_id_type=MESH
            )
        return body

    every(nh, greet(head_peer, at_head))
    every(nx, greet(x_peer, at_x))
    every(NZ, greet(z_peer, at_z))
    loads[0].wait()
    maskbuf[head] = jnp.zeros((1, 384), F32)
    maskbuf[head, :, 0:piece] = (mask_ref[...] > 0).astype(F32).reshape(1, piece)
    pl.semaphore_wait(barrier, nh + nx + NZ - 3)

    every(nh, lambda i: send(
        maskbuf.at[head], maskbuf.at[head], m_send, m_recv, at_head(head_peer(i))
    ).start())

    loads[1].wait()
    loads[2].wait()
    lat_key = lk_ref[...]

    def dec_probs(i, carry):
        span = pl.ds(pl.multiple_of(i * size, size), size)
        score = dot(pq_ref[span, :], lat_key, NT) * scale
        e = jnp.exp(score - jnp.max(score, axis=1, keepdims=True))
        dprob[span, :] = e * (1.0 / jnp.sum(e, axis=1, keepdims=True))
        return carry

    lax.fori_loop(0, chunks, dec_probs, 0)

    mask_all = all_of(maskbuf, nh, m_send, m_recv, at_head(head_peer(1)))
    mask_all.wait_recv()
    for h in range(nh):
        line = jnp.broadcast_to(maskbuf[h], (128, 384))
        mcol[h * piece:(h + 1) * piece, :] = line.T[:piece, :]

    loads[3].wait()
    loads[4].wait()
    lat_value = lv_ref[...]

    def dec_grads(i, carry):
        span = pl.ds(pl.multiple_of(i * size, size), size)
        masked = dg_ref[span, :] * mcol[span, :].astype(BF16)
        dg = dot(masked, lat_value, NT)
        p = dprob[span, :]
        dd = jnp.sum(p * dg, axis=1, keepdims=True)
        ds = (p * (dg - dd)).astype(BF16)
        gpq_ref[span, :] = (dot(ds, lat_key, NN) * scale).astype(BF16)
        key_t, value_t = carry
        key_t = key_t + dot(pq_ref[span, :], ds, TN)
        value_t = value_t + dot(masked, p.astype(BF16), TN)
        return key_t, value_t

    blank = jnp.zeros((DH, LAT), F32)
    key_t, value_t = lax.fori_loop(0, chunks, dec_grads, (blank, blank))
    pdec[0:nx // 2] = key_t.T.reshape(nx // 2, NZ, 8, 128)
    pdec[nx // 2:nx] = value_t.T.reshape(nx // 2, NZ, 8, 128)

    class Sum:
        def __init__(self, part, rx, summed, rz, full, *sems):
            self.part, self.rx, self.summed, self.rz, self.full = part, rx, summed, rz, full
            self.x_sems, self.z_sems = sems[0:2], sems[2:4]
            self.az_sems, self.ax_sems = sems[4:6], sems[6:8]
            self.whole = [
                all_of(rx, nx, *self.x_sems, at_x(x_peer(1))),
                all_of(rz, NZ, *self.z_sems, at_z(z_peer(1))),
                all_of(full.at[xi], NZ, *self.az_sems, at_z(z_peer(1))),
                all_of(full, nx, *self.ax_sems, at_x(x_peer(1))),
            ]

        def scatter_x(self):
            every(nx, lambda i: send(
                self.part.at[x_peer(i)], self.rx.at[xi], *self.x_sems, at_x(x_peer(i))
            ).start())

        def gathered_x(self):
            self.rx[xi] = self.part[xi]
            self.whole[0].wait_recv()

        def scatter_z(self):
            every(NZ, lambda i: send(
                self.summed.at[z_peer(i)], self.rz.at[zi], *self.z_sems, at_z(z_peer(i))
            ).start())

        def gather_z(self):
            self.rz[zi] = self.summed[zi]
            self.whole[1].wait_recv()
            pieces = [self.rz[i] for i in range(NZ)]
            while len(pieces) > 1:
                pieces = [a + b for a, b in zip(pieces[0::2], pieces[1::2])]
            self.full[xi, zi] = pieces[0]
            every(NZ, lambda i: send(
                self.full.at[xi, zi], self.full.at[xi, zi], *self.az_sems, at_z(z_peer(i))
            ).start())

        def gather_x(self):
            self.whole[2].wait_recv()
            every(nx, lambda i: send(
                self.full.at[xi], self.full.at[xi], *self.ax_sems, at_x(x_peer(i))
            ).start())

        def finish(self):
            self.whole[3].wait_recv()

        def drain(self):
            for copy in self.whole:
                copy.wait_send()

    dec = Sum(
        pdec, rxdec, sumdec, rzdec, fulldec,
        dx_send, dx_recv, dz_send, dz_recv, daz_send, daz_recv, dax_send, dax_recv,
    )
    enc = Sum(
        pq, rxq, sumq, rzq, fullq,
        qx_send, qx_recv, qz_send, qz_recv, qaz_send, qaz_recv, qax_send, qax_recv,
    )
    dec.scatter_x()

    for load in loads[5:]:
        load.wait()
    lat_query = lq_ref[...]
    enc_grad = eg_ref[...]

    def enc_first(i, carry):
        top, total, delta, a, b = carry
        span = pl.ds(pl.multiple_of(i * size, size), size)
        keys = pk_ref[span, :]
        bias = (mcol[span, :] - 1.0) * 1e30
        score = dot(keys, lat_query, NT) * scale
        score = score + jnp.concatenate([bias, bias], axis=1)
        grad = dot(pv_ref[span, :], enc_grad, NT)
        own = jnp.max(score, axis=0, keepdims=True)
        e = jnp.exp(score - own)
        expo[span, :] = e
        edot[span, :] = grad
        chunk_top[i] = own
        own_total = jnp.sum(e, axis=0, keepdims=True)
        own_delta = jnp.sum(e * grad, axis=0, keepdims=True) / own_total
        ds = (e * (grad - own_delta)).astype(BF16)
        sums = dot(keys, jnp.concatenate([ds, e.astype(BF16)], axis=1), TN)
        own_a, own_b = sums[:, :LAT], sums[:, LAT:]
        later = jnp.maximum(top, own)
        left = jnp.exp(top - later)
        right = jnp.exp(own - later)
        both = total * left + own_total * right
        mixed = (total * left * delta + own_total * right * own_delta) / both
        a = left * (a + (delta - mixed) * b) + right * (own_a + (own_delta - mixed) * own_b)
        b = left * b + right * own_b
        return later, both, mixed, a, b

    zero = jnp.zeros((1, LAT), F32)
    top, total, delta, a, b = lax.fori_loop(
        0, chunks, enc_first, (jnp.full((1, LAT), -3e30, F32), zero, zero, blank, blank)
    )

    def put_stats(ref, slot, lse_rows, delta_rows):
        ref[slot, 0:2, :] = lse_rows
        ref[slot, 2:4, :] = delta_rows

    put_stats(sx, xi, fold(top + jnp.log(total)), fold(delta))
    every(nx, lambda i: send(sx.at[xi], sx.at[xi], sx_send, sx_recv, at_x(x_peer(i))).start())

    share = 1.0 / total
    a = a * share
    b = b * share

    def place(i, j):
        at = i * (DH // nx) + (j // 2) * 4
        return slice(at, at + 4), slice((j % 2) * 128, (j % 2) * 128 + 128)

    for i in range(nx):
        for j in range(NZ):
            pq[i, j] = jnp.concatenate([a[place(i, j)], b[place(i, j)]], axis=0)
    enc.scatter_x()

    sx_all = all_of(sx, nx, sx_send, sx_recv, at_x(x_peer(1)))
    sx_all.wait_recv()
    put_stats(sz, zi, *merge_stats(sx, nx))
    every(NZ, lambda i: send(sz.at[zi], sz.at[zi], sz_send, sz_recv, at_z(z_peer(i))).start())

    dec.gathered_x()
    sumdec[...] = (rxdec[0] + rxdec[1]) + (rxdec[2] + rxdec[3])
    dec.scatter_z()

    sz_all = all_of(sz, NZ, sz_send, sz_recv, at_z(z_peer(1)))
    sz_all.wait_recv()
    lse2, delta2 = merge_stats(sz, NZ)
    enc.gathered_x()
    factors = [jnp.exp(sx[i, 0:2, :] - lse2) for i in range(nx)]
    shifts = [sx[i, 2:4, :] - delta2 for i in range(nx)]
    for j in range(NZ):
        half = slice(j % 2, j % 2 + 1)
        terms = [
            factors[i][half] * (rxq[i, j, 0:4, :] + shifts[i][half] * rxq[i, j, 4:8, :])
            for i in range(nx)
        ]
        sumq[j] = functools.reduce(jnp.add, terms)
    enc.scatter_z()

    lse = jnp.concatenate([lse2[0:1], lse2[1:2]], axis=1)
    delta = jnp.concatenate([delta2[0:1], delta2[1:2]], axis=1)

    def enc_packets(i, carry):
        span = pl.ds(pl.multiple_of(i * size, size), size)
        p = expo[span, :] * jnp.exp(chunk_top[i] - lse)
        ds = (p * (edot[span, :] - delta)).astype(BF16)
        gpk_ref[span, :] = (dot(ds, lat_query, NN) * scale).astype(BF16)
        gpv_ref[span, :] = dot(p.astype(BF16), enc_grad, NN).astype(BF16)
        return carry

    lax.fori_loop(0, chunks // 2, enc_packets, 0)
    dec.gather_z()
    enc.gather_z()
    lax.fori_loop(chunks // 2, chunks, enc_packets, 0)
    dec.gather_x()
    enc.gather_x()
    dec.finish()
    glk_ref[...] = (fulldec[0:nx // 2].reshape(LAT, DH) * scale).astype(BF16)
    glv_ref[...] = fulldec[nx // 2:nx].reshape(LAT, DH)
    enc.finish()
    for i in range(nx):
        for k in range(0, NZ, 4):
            for c in range(2):
                at, lanes = place(i, k + c)
                query_t[at.start:at.start + 8, lanes] = jnp.concatenate(
                    [fullq[i, k + c], fullq[i, k + 2 + c]], axis=0
                )
    glq_ref[...] = (query_t[...].T * scale).astype(BF16)

    mask_all.wait_send()
    sx_all.wait_send()
    sz_all.wait_send()
    dec.drain()
    enc.drain()


def write_out(*refs):
    count = len(refs) // 2
    sems = refs[-1]
    copies = [
        pltpu.make_async_copy(refs[i], refs[count + i], sems.at[i]) for i in range(count)
    ]
    for copy in copies:
        copy.start()
    for copy in copies:
        copy.wait()


def solution(mesh):
    nx = mesh.shape["seq"] // NZ
    nh = mesh.shape["head"]

    def on_device(lq, pk, pv, eg, pq, lk, lv, dg, mask):
        rows = pk.shape[0]
        vmem = pl.BlockSpec(memory_space=pltpu.VMEM)
        hbm = pl.BlockSpec(memory_space=pltpu.HBM)
        lat = jax.ShapeDtypeStruct((LAT, DH), BF16)
        pkt = jax.ShapeDtypeStruct((rows, DH), BF16)
        outs = (lat, pkt, pkt, pkt, lat, jax.ShapeDtypeStruct((LAT, DH), F32))
        args = [
            pltpu.with_memory_space_constraint(x, pltpu.HBM)
            for x in (lq, pk, pv, eg, pq, lk, lv, dg, mask)
        ]

        def reduce_buffers(sent, depth):
            return [
                pltpu.VMEM((nx, NZ, sent, 128), F32),
                pltpu.VMEM((nx, NZ, sent, 128), F32),
                pltpu.VMEM((NZ, depth, 128), F32),
                pltpu.VMEM((NZ, depth, 128), F32),
                pltpu.VMEM((nx, NZ, depth, 128), F32),
            ]

        made = pl.pallas_call(
            functools.partial(kernel, nx, nh, rows),
            out_shape=outs,
            in_specs=[hbm] * len(args),
            out_specs=(vmem,) * len(outs),
            scratch_shapes=[pltpu.VMEM(x.shape, x.dtype) for x in args]
            + [
                pltpu.VMEM((nh, 1, 384), F32),
                pltpu.VMEM((rows, 128), F32),
                pltpu.VMEM((rows, LAT), F32),
                pltpu.VMEM((rows, LAT), F32),
                pltpu.VMEM((4, 1, LAT), F32),
                pltpu.VMEM((rows, LAT), F32),
                pltpu.VMEM((DH, LAT), F32),
                pltpu.VMEM((nx, 4, 128), F32),
                pltpu.VMEM((NZ, 4, 128), F32),
            ]
            + reduce_buffers(8, 8)
            + reduce_buffers(8, 4)
            + [pltpu.SemaphoreType.DMA((len(args),))]
            + [pltpu.SemaphoreType.DMA((1,))] * 22,
            compiler_params=pltpu.CompilerParams(
                collective_id=0, has_side_effects=True, vmem_limit_bytes=48 * 2**20
            ),
            name="perceiver_backward",
        )(*args)
        return pl.pallas_call(
            write_out,
            out_shape=outs,
            in_specs=[vmem] * len(outs),
            out_specs=(hbm,) * len(outs),
            scratch_shapes=[pltpu.SemaphoreType.DMA((len(outs),))],
            name="write_out",
        )(*made)

    return jax.shard_map(
        on_device,
        mesh=mesh,
        in_specs=(
            P(None, "head"),
            P("seq", "head"),
            P("seq", "head"),
            P(None, "head"),
            P("seq", "head"),
            P(None, "head"),
            P(None, "head"),
            P("seq", "head"),
            P(("seq", "head")),
        ),
        out_specs=(
            P(None, "head"),
            P("seq", "head"),
            P("seq", "head"),
            P("seq", "head"),
            P(None, "head"),
            P(None, "head"),
        ),
        check_vma=False,
    )
```

```python
import functools
import math

import jax
import jax.numpy as jnp
from jax import lax
from jax.experimental import pallas as pl
from jax.experimental.pallas import tpu as pltpu
from jax.sharding import PartitionSpec as P

DH = 128
LAT = 256
NZ = 16
MESH = pl.DeviceIdType.MESH
F32 = jnp.float32
BF16 = jnp.bfloat16
NT = (((1,), (1,)), ((), ()))
NN = (((1,), (0,)), ((), ()))
TN = (((0,), (0,)), ((), ()))


def dot(a, b, dims):
    return lax.dot_general(a, b, dims, preferred_element_type=F32)


def merge_stats(ref, count):
    lses = [ref[i, 0:2, :] for i in range(count)]
    top = functools.reduce(jnp.maximum, lses)
    weights = [jnp.exp(lse - top) for lse in lses]
    total = functools.reduce(jnp.add, weights)
    mixed = functools.reduce(jnp.add, [w * ref[i, 2:4, :] for i, w in enumerate(weights)])
    return top + jnp.log(total), mixed / total


def fold(line):
    return jnp.concatenate([line[:, :128], line[:, 128:]], axis=0)


def kernel(
    nx, nh, rows,
    lq_hbm, pk_hbm, pv_hbm, eg_hbm, pq_hbm, lk_hbm, lv_hbm, dg_hbm, mask_hbm,
    glq_ref, gpk_ref, gpv_ref, gpq_ref, glk_ref, glv_ref,
    lq_ref, pk_ref, pv_ref, eg_ref, pq_ref, lk_ref, lv_ref, dg_ref, mask_ref,
    maskbuf, mcol, expo, edot, esums, dprob, dscore, query_t,
    sx, sz, pdec, rxdec, sumdec, rzdec, fulldec, pq, rxq, sumq, rzq, fullq,
    in_sems,
    m_send, m_recv, sx_send, sx_recv, sz_send, sz_recv,
    dx_send, dx_recv, dz_send, dz_recv, daz_send, daz_recv, dax_send, dax_recv,
    qx_send, qx_recv, qz_send, qz_recv, qaz_send, qaz_recv, qax_send, qax_recv,
):
    scale = 1.0 / math.sqrt(DH)
    piece = rows // nh
    size = 384
    spans = [slice(at, at + size) for at in range(0, rows, size)]
    seq = lax.axis_index("seq")
    head = lax.axis_index("head")
    xi = seq // NZ
    zi = lax.rem(seq, NZ)

    loads = [
        pltpu.make_async_copy(src, dst, in_sems.at[i])
        for i, (src, dst) in enumerate(
            (
                (mask_hbm, mask_ref),
                (pq_hbm, pq_ref),
                (lk_hbm, lk_ref),
                (dg_hbm, dg_ref),
                (lv_hbm, lv_ref),
                (pk_hbm, pk_ref),
                (lq_hbm, lq_ref),
                (pv_hbm, pv_ref),
                (eg_hbm, eg_ref),
            )
        )
    ]
    for load in loads:
        load.start()

    def head_peer(step):
        return lax.rem(head + step, nh)

    def x_peer(step):
        return lax.rem(xi + step, nx)

    def z_peer(step):
        return lax.rem(zi + NZ // 2 + (step // 2) * (2 * lax.rem(step, 2) - 1), NZ)

    def at_head(peer):
        return (seq, peer)

    def at_x(peer):
        return (peer * NZ + zi, head)

    def at_z(peer):
        return (xi * NZ + peer, head)

    def every(count, body):
        def step(i, carry):
            body(i)
            return carry

        lax.fori_loop(1, count, step, 0)

    def send(src, dst, send_sem, recv_sem, target):
        return pltpu.make_async_remote_copy(
            src_ref=src, dst_ref=dst, send_sem=send_sem.at[0], recv_sem=recv_sem.at[0],
            device_id=target, device_id_type=MESH,
        )

    def all_of(ref, count, send_sem, recv_sem, target):
        part = ref.at[pl.ds(0, count - 1)]
        return send(part, part, send_sem, recv_sem, target)

    barrier = pltpu.get_barrier_semaphore()

    def greet(peer_of, place):
        def body(step):
            pl.semaphore_signal(
                barrier, inc=1, device_id=place(peer_of(step)), device_id_type=MESH
            )
        return body

    every(nh, greet(head_peer, at_head))
    every(nx, greet(x_peer, at_x))
    every(NZ, greet(z_peer, at_z))
    loads[0].wait()
    maskbuf[head] = jnp.zeros((1, 384), F32)
    maskbuf[head, :, 0:piece] = (mask_ref[...] > 0).astype(F32).reshape(1, piece)
    pl.semaphore_wait(barrier, nh + nx + NZ - 3)

    every(nh, lambda i: send(
        maskbuf.at[head], maskbuf.at[head], m_send, m_recv, at_head(head_peer(i))
    ).start())

    for load in loads[1:5]:
        load.wait()
    lat_key = lk_ref[...]
    lat_value = lv_ref[...]
    for span in spans:
        score = dot(lat_key, pq_ref[span, :], NT) * scale
        e = jnp.exp(score - jnp.max(score, axis=0, keepdims=True))
        p = e * (1.0 / jnp.sum(e, axis=0, keepdims=True))
        dg = dot(lat_value, dg_ref[span, :], NT)
        dd = jnp.sum(p * dg, axis=0, keepdims=True)
        dprob[:, span] = p.astype(BF16)
        dscore[:, span] = (p * (dg - dd)).astype(BF16)

    mask_all = all_of(maskbuf, nh, m_send, m_recv, at_head(head_peer(1)))
    mask_all.wait_recv()
    for h in range(nh):
        line = jnp.broadcast_to(maskbuf[h], (128, 384))
        mcol[h * piece:(h + 1) * piece, :] = line.T[:piece, :]

    class Sum:
        def __init__(self, part, rx, summed, rz, full, *sems):
            self.part, self.rx, self.summed, self.rz, self.full = part, rx, summed, rz, full
            self.x_sems, self.z_sems = sems[0:2], sems[2:4]
            self.az_sems, self.ax_sems = sems[4:6], sems[6:8]
            self.whole = [
                all_of(rx, nx, *self.x_sems, at_x(x_peer(1))),
                all_of(rz, NZ, *self.z_sems, at_z(z_peer(1))),
                all_of(full.at[xi], NZ, *self.az_sems, at_z(z_peer(1))),
                all_of(full, nx, *self.ax_sems, at_x(x_peer(1))),
            ]

        def scatter_x(self):
            every(nx, lambda i: send(
                self.part.at[x_peer(i)], self.rx.at[xi], *self.x_sems, at_x(x_peer(i))
            ).start())

        def gathered_x(self):
            self.rx[xi] = self.part[xi]
            self.whole[0].wait_recv()

        def scatter_z(self):
            every(NZ, lambda i: send(
                self.summed.at[z_peer(i)], self.rz.at[zi], *self.z_sems, at_z(z_peer(i))
            ).start())

        def gather_z(self):
            self.rz[zi] = self.summed[zi]
            self.whole[1].wait_recv()
            pieces = [self.rz[i] for i in range(NZ)]
            while len(pieces) > 1:
                pieces = [a + b for a, b in zip(pieces[0::2], pieces[1::2])]
            self.full[xi, zi] = pieces[0]
            every(NZ, lambda i: send(
                self.full.at[xi, zi], self.full.at[xi, zi], *self.az_sems, at_z(z_peer(i))
            ).start())

        def gather_x(self):
            self.whole[2].wait_recv()
            every(nx, lambda i: send(
                self.full.at[xi], self.full.at[xi], *self.ax_sems, at_x(x_peer(i))
            ).start())

        def finish(self):
            self.whole[3].wait_recv()

        def drain(self):
            for copy in self.whole:
                copy.wait_send()

    dec = Sum(
        pdec, rxdec, sumdec, rzdec, fulldec,
        dx_send, dx_recv, dz_send, dz_recv, daz_send, daz_recv, dax_send, dax_recv,
    )
    enc = Sum(
        pq, rxq, sumq, rzq, fullq,
        qx_send, qx_recv, qz_send, qz_recv, qaz_send, qaz_recv, qax_send, qax_recv,
    )
    for load in loads[5:]:
        load.wait()
    lat_query = lq_ref[...]
    enc_grad = eg_ref[...]
    tops, totals, deltas = [], [], []
    for span in spans:
        bias = (mcol[span, :] - 1.0) * 1e30
        score = dot(pk_ref[span, :], lat_query, NT) * scale
        score = score + jnp.concatenate([bias, bias], axis=1)
        grad = dot(pv_ref[span, :], enc_grad, NT)
        own = jnp.max(score, axis=0, keepdims=True)
        e = jnp.exp(score - own)
        expo[span, :] = e
        edot[span, :] = grad
        own_total = jnp.sum(e, axis=0, keepdims=True)
        own_delta = jnp.sum(e * grad, axis=0, keepdims=True) / own_total
        esums[span, :LAT] = (e * (grad - own_delta)).astype(BF16)
        esums[span, LAT:] = e.astype(BF16)
        tops.append(own)
        totals.append(own_total)
        deltas.append(own_delta)
    top = functools.reduce(jnp.maximum, tops)
    shares = [jnp.exp(own - top) for own in tops]
    weights = [w * t for w, t in zip(shares, totals)]
    total = functools.reduce(jnp.add, weights)
    inverse = 1.0 / total
    delta = functools.reduce(jnp.add, [w * d for w, d in zip(weights, deltas)]) * inverse

    def put_stats(ref, slot, lse_rows, delta_rows):
        ref[slot, 0:2, :] = lse_rows
        ref[slot, 2:4, :] = delta_rows

    put_stats(sx, xi, fold(top + jnp.log(total)), fold(delta))
    every(nx, lambda i: send(sx.at[xi], sx.at[xi], sx_send, sx_recv, at_x(x_peer(i))).start())

    key_sum = jnp.zeros((LAT, DH), F32)
    value_sum = jnp.zeros((LAT, DH), F32)
    for span in spans:
        valid = mcol[span, :].astype(BF16)
        key_sum = key_sum + dot(dscore[:, span], pq_ref[span, :] * valid, NN)
        value_sum = value_sum + dot(dprob[:, span], dg_ref[span, :] * valid, NN)
    pdec[0:nx // 2] = key_sum.reshape(nx // 2, NZ, 8, 128)
    pdec[nx // 2:nx] = value_sum.reshape(nx // 2, NZ, 8, 128)
    dec.scatter_x()

    sx_all = all_of(sx, nx, sx_send, sx_recv, at_x(x_peer(1)))
    sx_all.wait_recv()
    put_stats(sz, zi, *merge_stats(sx, nx))
    every(NZ, lambda i: send(sz.at[zi], sz.at[zi], sz_send, sz_recv, at_z(z_peer(i))).start())

    a = jnp.zeros((DH, LAT), F32)
    b = jnp.zeros((DH, LAT), F32)
    for span, w, d in zip(spans, shares, deltas):
        sums = dot(pk_ref[span, :], esums[span, :], TN)
        w = w * inverse
        a = a + w * (sums[:, :LAT] + (d - delta) * sums[:, LAT:])
        b = b + w * sums[:, LAT:]

    def place(i, j):
        at = i * (DH // nx) + (j // 2) * 4
        return slice(at, at + 4), slice((j % 2) * 128, (j % 2) * 128 + 128)

    for i in range(nx):
        for j in range(NZ):
            pq[i, j] = jnp.concatenate([a[place(i, j)], b[place(i, j)]], axis=0)
    enc.scatter_x()

    for span in spans:
        grad = dot(dscore[:, span], lat_key, TN) * (mcol[span, :] * scale)
        gpq_ref[span, :] = grad.astype(BF16)

    dec.gathered_x()
    sumdec[...] = (rxdec[0] + rxdec[1]) + (rxdec[2] + rxdec[3])
    dec.scatter_z()

    sz_all = all_of(sz, NZ, sz_send, sz_recv, at_z(z_peer(1)))
    sz_all.wait_recv()
    lse2, delta2 = merge_stats(sz, NZ)
    enc.gathered_x()
    factors = [jnp.exp(sx[i, 0:2, :] - lse2) for i in range(nx)]
    shifts = [sx[i, 2:4, :] - delta2 for i in range(nx)]
    for j in range(NZ):
        half = slice(j % 2, j % 2 + 1)
        terms = [
            factors[i][half] * (rxq[i, j, 0:4, :] + shifts[i][half] * rxq[i, j, 4:8, :])
            for i in range(nx)
        ]
        sumq[j] = functools.reduce(jnp.add, terms)
    enc.scatter_z()

    lse = jnp.concatenate([lse2[0:1], lse2[1:2]], axis=1)
    delta = jnp.concatenate([delta2[0:1], delta2[1:2]], axis=1)

    def enc_packets(first, last):
        for span, own in zip(spans[first:last], tops[first:last]):
            p = expo[span, :] * jnp.exp(own - lse)
            ds = (p * (edot[span, :] - delta)).astype(BF16)
            gpk_ref[span, :] = (dot(ds, lat_query, NN) * scale).astype(BF16)
            gpv_ref[span, :] = dot(p.astype(BF16), enc_grad, NN).astype(BF16)

    enc_packets(0, 3)
    dec.gather_z()
    enc_packets(3, len(spans))
    enc.gather_z()
    dec.gather_x()
    enc.gather_x()
    dec.finish()
    glk_ref[...] = (fulldec[0:nx // 2].reshape(LAT, DH) * scale).astype(BF16)
    glv_ref[...] = fulldec[nx // 2:nx].reshape(LAT, DH)
    enc.finish()
    for i in range(nx):
        for k in range(0, NZ, 4):
            for c in range(2):
                at, lanes = place(i, k + c)
                query_t[at.start:at.start + 8, lanes] = jnp.concatenate(
                    [fullq[i, k + c], fullq[i, k + 2 + c]], axis=0
                )
    glq_ref[...] = (query_t[...].T * scale).astype(BF16)

    mask_all.wait_send()
    sx_all.wait_send()
    sz_all.wait_send()
    dec.drain()
    enc.drain()


def write_out(*refs):
    count = len(refs) // 2
    sems = refs[-1]
    copies = [
        pltpu.make_async_copy(refs[i], refs[count + i], sems.at[i]) for i in range(count)
    ]
    for copy in copies:
        copy.start()
    for copy in copies:
        copy.wait()


def solution(mesh):
    nx = mesh.shape["seq"] // NZ
    nh = mesh.shape["head"]

    def on_device(lq, pk, pv, eg, pq, lk, lv, dg, mask):
        rows = pk.shape[0]
        vmem = pl.BlockSpec(memory_space=pltpu.VMEM)
        hbm = pl.BlockSpec(memory_space=pltpu.HBM)
        lat = jax.ShapeDtypeStruct((LAT, DH), BF16)
        pkt = jax.ShapeDtypeStruct((rows, DH), BF16)
        outs = (lat, pkt, pkt, pkt, lat, jax.ShapeDtypeStruct((LAT, DH), F32))
        args = [
            pltpu.with_memory_space_constraint(x, pltpu.HBM)
            for x in (lq, pk, pv, eg, pq, lk, lv, dg, mask)
        ]

        def reduce_buffers(sent, depth):
            return [
                pltpu.VMEM((nx, NZ, sent, 128), F32),
                pltpu.VMEM((nx, NZ, sent, 128), F32),
                pltpu.VMEM((NZ, depth, 128), F32),
                pltpu.VMEM((NZ, depth, 128), F32),
                pltpu.VMEM((nx, NZ, depth, 128), F32),
            ]

        made = pl.pallas_call(
            functools.partial(kernel, nx, nh, rows),
            out_shape=outs,
            in_specs=[hbm] * len(args),
            out_specs=(vmem,) * len(outs),
            scratch_shapes=[pltpu.VMEM(x.shape, x.dtype) for x in args]
            + [
                pltpu.VMEM((nh, 1, 384), F32),
                pltpu.VMEM((rows, 128), F32),
                pltpu.VMEM((rows, LAT), F32),
                pltpu.VMEM((rows, LAT), F32),
                pltpu.VMEM((rows, 2 * LAT), BF16),
                pltpu.VMEM((LAT, rows), BF16),
                pltpu.VMEM((LAT, rows), BF16),
                pltpu.VMEM((DH, LAT), F32),
                pltpu.VMEM((nx, 4, 128), F32),
                pltpu.VMEM((NZ, 4, 128), F32),
            ]
            + reduce_buffers(8, 8)
            + reduce_buffers(8, 4)
            + [pltpu.SemaphoreType.DMA((len(args),))]
            + [pltpu.SemaphoreType.DMA((1,))] * 22,
            compiler_params=pltpu.CompilerParams(
                collective_id=0, has_side_effects=True, vmem_limit_bytes=48 * 2**20
            ),
            name="perceiver_backward",
        )(*args)
        return pl.pallas_call(
            write_out,
            out_shape=outs,
            in_specs=[vmem] * len(outs),
            out_specs=(hbm,) * len(outs),
            scratch_shapes=[pltpu.SemaphoreType.DMA((len(outs),))],
            compiler_params=pltpu.CompilerParams(vmem_limit_bytes=2**20),
            name="write_out",
        )(*[pltpu.with_memory_space_constraint(x, pltpu.VMEM) for x in made])

    return jax.shard_map(
        on_device,
        mesh=mesh,
        in_specs=(
            P(None, "head"),
            P("seq", "head"),
            P("seq", "head"),
            P(None, "head"),
            P("seq", "head"),
            P(None, "head"),
            P(None, "head"),
            P("seq", "head"),
            P(("seq", "head")),
        ),
        out_specs=(
            P(None, "head"),
            P("seq", "head"),
            P("seq", "head"),
            P("seq", "head"),
            P(None, "head"),
            P(None, "head"),
        ),
        check_vma=False,
    )
```

```python
import functools
import math

import jax
import jax.numpy as jnp
from jax import lax
from jax.experimental import pallas as pl
from jax.experimental.pallas import tpu as pltpu
from jax.sharding import PartitionSpec as P

DH = 128
LAT = 256
NZ = 16
MESH = pl.DeviceIdType.MESH
F32 = jnp.float32
BF16 = jnp.bfloat16
NT = (((1,), (1,)), ((), ()))
NN = (((1,), (0,)), ((), ()))
TN = (((0,), (0,)), ((), ()))


def dot(a, b, dims):
    return lax.dot_general(a, b, dims, preferred_element_type=F32)


def merge_stats(ref, count):
    lses = [ref[i, 0:2, :] for i in range(count)]
    top = functools.reduce(jnp.maximum, lses)
    weights = [jnp.exp(lse - top) for lse in lses]
    total = functools.reduce(jnp.add, weights)
    mixed = functools.reduce(jnp.add, [w * ref[i, 2:4, :] for i, w in enumerate(weights)])
    return top + jnp.log(total), mixed / total


def tree_sum(pieces):
    while len(pieces) > 1:
        pieces = [a + b for a, b in zip(pieces[0::2], pieces[1::2])]
    return pieces[0]


def fold(line):
    return jnp.concatenate([line[:, :128], line[:, 128:]], axis=0)


def kernel(
    nx, nh, rows,
    lq_hbm, pk_hbm, pv_hbm, eg_hbm, pq_hbm, lk_hbm, lv_hbm, dg_hbm, mask_hbm,
    glq_ref, gpk_ref, gpv_ref, gpq_ref, glk_ref, glv_ref,
    lq_ref, pk_ref, pv_ref, eg_ref, pq_ref, lk_ref, lv_ref, dg_ref, mask_ref,
    maskbuf, mcol, expo, edot, esums, dprob, dscore, query_t,
    sx, sz, pdec, rxdec, sumdec, rzdec, fulldec, pq, rxq, sumq, rzq, fullq,
    in_sems,
    m_send, m_recv, sx_send, sx_recv, sz_send, sz_recv,
    dx_send, dx_recv, dz_send, dz_recv, daz_send, daz_recv, dax_send, dax_recv,
    qx_send, qx_recv, qz_send, qz_recv, qaz_send, qaz_recv, qax_send, qax_recv,
):
    scale = 1.0 / math.sqrt(DH)
    piece = rows // nh
    size = 384
    spans = [slice(at, at + size) for at in range(0, rows, size)]
    seq = lax.axis_index("seq")
    head = lax.axis_index("head")
    xi = seq // NZ
    zi = lax.rem(seq, NZ)

    loads = [
        pltpu.make_async_copy(src, dst, in_sems.at[i])
        for i, (src, dst) in enumerate(
            (
                (mask_hbm, mask_ref),
                (pq_hbm, pq_ref),
                (lk_hbm, lk_ref),
                (dg_hbm, dg_ref),
                (lv_hbm, lv_ref),
                (pk_hbm, pk_ref),
                (lq_hbm, lq_ref),
                (pv_hbm, pv_ref),
                (eg_hbm, eg_ref),
            )
        )
    ]
    for load in loads:
        load.start()

    def head_peer(step):
        return lax.rem(head + step, nh)

    def x_peer(step):
        return lax.rem(xi + step, nx)

    def z_peer(step):
        return lax.rem(zi + NZ // 2 + (step // 2) * (2 * lax.rem(step, 2) - 1), NZ)

    def at_head(peer):
        return (seq, peer)

    def at_x(peer):
        return (peer * NZ + zi, head)

    def at_z(peer):
        return (xi * NZ + peer, head)

    def every(count, body):
        def step(i, carry):
            body(i)
            return carry

        lax.fori_loop(1, count, step, 0)

    def send(src, dst, send_sem, recv_sem, target):
        return pltpu.make_async_remote_copy(
            src_ref=src, dst_ref=dst, send_sem=send_sem.at[0], recv_sem=recv_sem.at[0],
            device_id=target, device_id_type=MESH,
        )

    def all_of(ref, count, send_sem, recv_sem, target):
        part = ref.at[pl.ds(0, count - 1)]
        return send(part, part, send_sem, recv_sem, target)

    barrier = pltpu.get_barrier_semaphore()

    def greet(peer_of, place):
        def body(step):
            pl.semaphore_signal(
                barrier, inc=1, device_id=place(peer_of(step)), device_id_type=MESH
            )
        return body

    every(nh, greet(head_peer, at_head))
    every(nx, greet(x_peer, at_x))
    every(NZ, greet(z_peer, at_z))
    loads[0].wait()
    maskbuf[head] = jnp.zeros((1, 384), F32)
    maskbuf[head, :, 0:piece] = (mask_ref[...] > 0).astype(F32).reshape(1, piece)
    def start_masks():
        pl.semaphore_wait(barrier, nh + nx + NZ - 3)

        every(nh, lambda i: send(
            maskbuf.at[head], maskbuf.at[head], m_send, m_recv, at_head(head_peer(i))
        ).start())

    for load in loads[1:5]:
        load.wait()
    lat_key = lk_ref[...]
    lat_value = lv_ref[...]
    for at, span in enumerate(spans):
        if at == len(spans) // 2:
            start_masks()
        score = dot(lat_key, pq_ref[span, :], NT) * scale
        e = jnp.exp(score - jnp.max(score, axis=0, keepdims=True))
        p = e * (1.0 / jnp.sum(e, axis=0, keepdims=True))
        dg = dot(lat_value, dg_ref[span, :], NT)
        dd = jnp.sum(p * dg, axis=0, keepdims=True)
        dprob[:, span] = p.astype(BF16)
        dscore[:, span] = (p * (dg - dd)).astype(BF16)

    mask_all = all_of(maskbuf, nh, m_send, m_recv, at_head(head_peer(1)))
    mask_all.wait_recv()
    for h in range(nh):
        line = jnp.broadcast_to(maskbuf[h], (128, 384))
        mcol[h * piece:(h + 1) * piece, :] = line.T[:piece, :]

    class Sum:
        def __init__(self, part, rx, summed, rz, full, *sems):
            self.part, self.rx, self.summed, self.rz, self.full = part, rx, summed, rz, full
            self.x_sems, self.z_sems = sems[0:2], sems[2:4]
            self.az_sems, self.ax_sems = sems[4:6], sems[6:8]
            self.whole = [
                all_of(rx, nx, *self.x_sems, at_x(x_peer(1))),
                all_of(rz, NZ, *self.z_sems, at_z(z_peer(1))),
                all_of(full.at[xi], NZ, *self.az_sems, at_z(z_peer(1))),
                all_of(full, nx, *self.ax_sems, at_x(x_peer(1))),
            ]

        def scatter_x(self):
            every(nx, lambda i: send(
                self.part.at[x_peer(i)], self.rx.at[xi], *self.x_sems, at_x(x_peer(i))
            ).start())

        def gathered_x(self):
            self.rx[xi] = self.part[xi]
            self.whole[0].wait_recv()

        def scatter_z(self):
            every(NZ, lambda i: send(
                self.summed.at[z_peer(i)], self.rz.at[zi], *self.z_sems, at_z(z_peer(i))
            ).start())

        def gather_z(self, join):
            self.rz[zi] = self.summed[zi]
            self.whole[1].wait_recv()
            self.full[xi, zi] = join([self.rz[i] for i in range(NZ)])
            every(NZ, lambda i: send(
                self.full.at[xi, zi], self.full.at[xi, zi], *self.az_sems, at_z(z_peer(i))
            ).start())

        def gather_x(self):
            self.whole[2].wait_recv()
            every(nx, lambda i: send(
                self.full.at[xi], self.full.at[xi], *self.ax_sems, at_x(x_peer(i))
            ).start())

        def finish(self):
            self.whole[3].wait_recv()

        def drain(self):
            for copy in self.whole:
                copy.wait_send()

    dec = Sum(
        pdec, rxdec, sumdec, rzdec, fulldec,
        dx_send, dx_recv, dz_send, dz_recv, daz_send, daz_recv, dax_send, dax_recv,
    )
    enc = Sum(
        pq, rxq, sumq, rzq, fullq,
        qx_send, qx_recv, qz_send, qz_recv, qaz_send, qaz_recv, qax_send, qax_recv,
    )
    key_sum = jnp.zeros((LAT, DH), F32)
    value_sum = jnp.zeros((LAT, DH), F32)
    for span in spans:
        valid = mcol[span, :].astype(BF16)
        key_sum = key_sum + dot(dscore[:, span], pq_ref[span, :] * valid, NN)
        value_sum = value_sum + dot(dprob[:, span], dg_ref[span, :] * valid, NN)
    pdec[0:nx // 2] = key_sum.reshape(nx // 2, NZ, 8, 128)
    pdec[nx // 2:nx] = value_sum.reshape(nx // 2, NZ, 8, 128)
    dec.scatter_x()

    for load in loads[5:]:
        load.wait()
    lat_query = lq_ref[...]
    enc_grad = eg_ref[...]
    tops, totals, deltas = [], [], []
    for span in spans:
        bias = (mcol[span, :] - 1.0) * 1e30
        score = dot(pk_ref[span, :], lat_query, NT) * scale
        score = score + jnp.concatenate([bias, bias], axis=1)
        grad = dot(pv_ref[span, :], enc_grad, NT)
        own = jnp.max(score, axis=0, keepdims=True)
        e = jnp.exp(score - own)
        expo[span, :] = e
        edot[span, :] = grad
        own_total = jnp.sum(e, axis=0, keepdims=True)
        own_delta = jnp.sum(e * grad, axis=0, keepdims=True) / own_total
        esums[span, :LAT] = (e * (grad - own_delta)).astype(BF16)
        esums[span, LAT:] = e.astype(BF16)
        tops.append(own)
        totals.append(own_total)
        deltas.append(own_delta)
    top = functools.reduce(jnp.maximum, tops)
    shares = [jnp.exp(own - top) for own in tops]
    weights = [w * t for w, t in zip(shares, totals)]
    total = functools.reduce(jnp.add, weights)
    inverse = 1.0 / total
    delta = functools.reduce(jnp.add, [w * d for w, d in zip(weights, deltas)]) * inverse

    def put_stats(ref, slot, lse_rows, delta_rows):
        ref[slot, 0:2, :] = lse_rows
        ref[slot, 2:4, :] = delta_rows

    put_stats(sx, xi, fold(top + jnp.log(total)), fold(delta))
    every(nx, lambda i: send(sx.at[xi], sx.at[xi], sx_send, sx_recv, at_x(x_peer(i))).start())

    dec.gathered_x()
    sumdec[...] = (rxdec[0] + rxdec[1]) + (rxdec[2] + rxdec[3])
    dec.scatter_z()

    a = jnp.zeros((DH, LAT), F32)
    b = jnp.zeros((DH, LAT), F32)
    for span, w, d in zip(spans, shares, deltas):
        sums = dot(pk_ref[span, :], esums[span, :], TN)
        w = w * inverse
        a = a + w * (sums[:, :LAT] + (d - delta) * sums[:, LAT:])
        b = b + w * sums[:, LAT:]

    def place(i, j):
        at = i * (DH // nx) + (j // 2) * 4
        return slice(at, at + 4), slice((j % 2) * 128, (j % 2) * 128 + 128)

    for i in range(nx):
        for j in range(NZ):
            pq[i, j] = jnp.concatenate([a[place(i, j)], b[place(i, j)]], axis=0)
    enc.scatter_x()

    sx_all = all_of(sx, nx, sx_send, sx_recv, at_x(x_peer(1)))
    sx_all.wait_recv()
    lse_x, delta_x = merge_stats(sx, nx)
    put_stats(sz, zi, lse_x, delta_x)
    every(NZ, lambda i: send(sz.at[zi], sz.at[zi], sz_send, sz_recv, at_z(z_peer(i))).start())

    for span in spans:
        grad = dot(dscore[:, span], lat_key, TN) * (mcol[span, :] * scale)
        gpq_ref[span, :] = grad.astype(BF16)

    dec.gather_z(tree_sum)

    def combine(factors, shifts, sums):
        a = functools.reduce(
            jnp.add, [f * (s[0:4] + d * s[4:8]) for f, d, s in zip(factors, shifts, sums)]
        )
        return a, functools.reduce(jnp.add, [f * s[4:8] for f, s in zip(factors, sums)])

    enc.gathered_x()
    factors = [jnp.exp(sx[i, 0:2, :] - lse_x) for i in range(nx)]
    shifts = [sx[i, 2:4, :] - delta_x for i in range(nx)]
    for j in range(NZ):
        half = slice(j % 2, j % 2 + 1)
        sumq[j] = jnp.concatenate(
            combine(
                [f[half] for f in factors],
                [d[half] for d in shifts],
                [rxq[i, j] for i in range(nx)],
            ),
            axis=0,
        )
    enc.scatter_z()

    sz_all = all_of(sz, NZ, sz_send, sz_recv, at_z(z_peer(1)))
    sz_all.wait_recv()
    lse2, delta2 = merge_stats(sz, NZ)
    lse = jnp.concatenate([lse2[0:1], lse2[1:2]], axis=1)
    delta = jnp.concatenate([delta2[0:1], delta2[1:2]], axis=1)

    def join_queries(sums):
        own_half = lax.rem(zi, 2) == 0

        def mine(lines):
            return jnp.where(own_half, lines[0:1], lines[1:2])

        return combine(
            [mine(jnp.exp(sz[i, 0:2, :] - lse2)) for i in range(NZ)],
            [mine(sz[i, 2:4, :] - delta2) for i in range(NZ)],
            sums,
        )[0]

    def enc_packets(first, last):
        for span, own in zip(spans[first:last], tops[first:last]):
            p = expo[span, :] * jnp.exp(own - lse)
            ds = (p * (edot[span, :] - delta)).astype(BF16)
            gpk_ref[span, :] = (dot(ds, lat_query, NN) * scale).astype(BF16)
            gpv_ref[span, :] = dot(p.astype(BF16), enc_grad, NN).astype(BF16)

    enc_packets(0, 3)
    dec.gather_x()
    enc.gather_z(join_queries)
    enc_packets(3, len(spans))
    enc.gather_x()
    dec.finish()
    glk_ref[...] = (fulldec[0:nx // 2].reshape(LAT, DH) * scale).astype(BF16)
    glv_ref[...] = fulldec[nx // 2:nx].reshape(LAT, DH)
    enc.finish()
    for i in range(nx):
        for k in range(0, NZ, 4):
            for c in range(2):
                at, lanes = place(i, k + c)
                query_t[at.start:at.start + 8, lanes] = jnp.concatenate(
                    [fullq[i, k + c], fullq[i, k + 2 + c]], axis=0
                )
    glq_ref[...] = (query_t[...].T * scale).astype(BF16)

    mask_all.wait_send()
    sx_all.wait_send()
    sz_all.wait_send()
    dec.drain()
    enc.drain()


def write_out(*refs):
    count = len(refs) // 2
    sems = refs[-1]
    copies = [
        pltpu.make_async_copy(refs[i], refs[count + i], sems.at[i]) for i in range(count)
    ]
    for copy in copies:
        copy.start()
    for copy in copies:
        copy.wait()


def solution(mesh):
    nx = mesh.shape["seq"] // NZ
    nh = mesh.shape["head"]

    def on_device(lq, pk, pv, eg, pq, lk, lv, dg, mask):
        rows = pk.shape[0]
        vmem = pl.BlockSpec(memory_space=pltpu.VMEM)
        hbm = pl.BlockSpec(memory_space=pltpu.HBM)
        lat = jax.ShapeDtypeStruct((LAT, DH), BF16)
        pkt = jax.ShapeDtypeStruct((rows, DH), BF16)
        outs = (lat, pkt, pkt, pkt, lat, jax.ShapeDtypeStruct((LAT, DH), F32))
        args = [
            pltpu.with_memory_space_constraint(x, pltpu.HBM)
            for x in (lq, pk, pv, eg, pq, lk, lv, dg, mask)
        ]

        def reduce_buffers(sent, depth):
            return [
                pltpu.VMEM((nx, NZ, sent, 128), F32),
                pltpu.VMEM((nx, NZ, sent, 128), F32),
                pltpu.VMEM((NZ, sent, 128), F32),
                pltpu.VMEM((NZ, sent, 128), F32),
                pltpu.VMEM((nx, NZ, depth, 128), F32),
            ]

        made = pl.pallas_call(
            functools.partial(kernel, nx, nh, rows),
            out_shape=outs,
            in_specs=[hbm] * len(args),
            out_specs=(vmem,) * len(outs),
            scratch_shapes=[pltpu.VMEM(x.shape, x.dtype) for x in args]
            + [
                pltpu.VMEM((nh, 1, 384), F32),
                pltpu.VMEM((rows, 128), F32),
                pltpu.VMEM((rows, LAT), F32),
                pltpu.VMEM((rows, LAT), F32),
                pltpu.VMEM((rows, 2 * LAT), BF16),
                pltpu.VMEM((LAT, rows), BF16),
                pltpu.VMEM((LAT, rows), BF16),
                pltpu.VMEM((DH, LAT), F32),
                pltpu.VMEM((nx, 4, 128), F32),
                pltpu.VMEM((NZ, 4, 128), F32),
            ]
            + reduce_buffers(8, 8)
            + reduce_buffers(8, 4)
            + [pltpu.SemaphoreType.DMA((len(args),))]
            + [pltpu.SemaphoreType.DMA((1,))] * 22,
            compiler_params=pltpu.CompilerParams(
                collective_id=0, has_side_effects=True, vmem_limit_bytes=48 * 2**20
            ),
            name="perceiver_backward",
        )(*args)
        return pl.pallas_call(
            write_out,
            out_shape=outs,
            in_specs=[vmem] * len(outs),
            out_specs=(hbm,) * len(outs),
            scratch_shapes=[pltpu.SemaphoreType.DMA((len(outs),))],
            compiler_params=pltpu.CompilerParams(vmem_limit_bytes=2**20),
            name="write_out",
        )(*[pltpu.with_memory_space_constraint(x, pltpu.VMEM) for x in made])

    return jax.shard_map(
        on_device,
        mesh=mesh,
        in_specs=(
            P(None, "head"),
            P("seq", "head"),
            P("seq", "head"),
            P(None, "head"),
            P("seq", "head"),
            P(None, "head"),
            P(None, "head"),
            P("seq", "head"),
            P(("seq", "head")),
        ),
        out_specs=(
            P(None, "head"),
            P("seq", "head"),
            P("seq", "head"),
            P("seq", "head"),
            P(None, "head"),
            P(None, "head"),
        ),
        check_vma=False,
    )
```

```python
import functools
import math

import jax
import jax.numpy as jnp
from jax import lax
from jax.experimental import pallas as pl
from jax.experimental.pallas import tpu as pltpu
from jax.sharding import PartitionSpec as P

DH = 128
LAT = 256
NZ = 16
MESH = pl.DeviceIdType.MESH
F32 = jnp.float32
BF16 = jnp.bfloat16
NT = (((1,), (1,)), ((), ()))
NN = (((1,), (0,)), ((), ()))
TN = (((0,), (0,)), ((), ()))


def dot(a, b, dims):
    return lax.dot_general(a, b, dims, preferred_element_type=F32)


def merge_stats(ref, count):
    lses = [ref[i, 0:2, :] for i in range(count)]
    top = functools.reduce(jnp.maximum, lses)
    weights = [jnp.exp(lse - top) for lse in lses]
    total = functools.reduce(jnp.add, weights)
    mixed = functools.reduce(jnp.add, [w * ref[i, 2:4, :] for i, w in enumerate(weights)])
    return top + jnp.log(total), mixed / total


def fold(line):
    return jnp.concatenate([line[:, :128], line[:, 128:]], axis=0)


def kernel(
    nx, nh, rows,
    lq_hbm, pk_hbm, pv_hbm, eg_hbm, pq_hbm, lk_hbm, lv_hbm, dg_hbm, mask_hbm,
    glq_ref, gpk_ref, gpv_ref, gpq_ref, glk_ref, glv_ref,
    lq_ref, pk_ref, pv_ref, eg_ref, pq_ref, lk_ref, lv_ref, dg_ref, mask_ref,
    maskbuf, mcol, expo, edot, esums, dprob, dscore, query_t,
    tops_ref, totals_ref, deltas_ref,
    sx, sz, pdec, rxdec, sumdec, rzdec, fulldec, pq, rxq, sumq, rzq, fullq,
    in_sems,
    m_send, m_recv, sx_send, sx_recv, sz_send, sz_recv,
    dx_send, dx_recv, dz_send, dz_recv, daz_send, daz_recv, dax_send, dax_recv,
    qx_send, qx_recv, qz_send, qz_recv, qaz_send, qaz_recv, qax_send, qax_recv,
):
    scale = 1.0 / math.sqrt(DH)
    piece = rows // nh
    size = 384
    steps, unroll = rows // size // 2, 2

    def chunks(first, last, body, carry=0):
        def step(i, carry):
            for k in range(unroll):
                at = i * unroll + k
                carry = body(at, pl.ds(pl.multiple_of(at * size, size), size), carry)
            return carry

        return lax.fori_loop(first, last, step, carry)
    seq = lax.axis_index("seq")
    head = lax.axis_index("head")
    xi = seq // NZ
    zi = lax.rem(seq, NZ)

    loads = [
        pltpu.make_async_copy(src, dst, in_sems.at[i])
        for i, (src, dst) in enumerate(
            (
                (mask_hbm, mask_ref),
                (pq_hbm, pq_ref),
                (lk_hbm, lk_ref),
                (dg_hbm, dg_ref),
                (lv_hbm, lv_ref),
                (pk_hbm, pk_ref),
                (lq_hbm, lq_ref),
                (pv_hbm, pv_ref),
                (eg_hbm, eg_ref),
            )
        )
    ]
    for load in loads:
        load.start()

    def head_peer(step):
        return lax.rem(head + step, nh)

    def x_peer(step):
        return lax.rem(xi + step, nx)

    def z_peer(step):
        return lax.rem(zi + NZ // 2 + (step // 2) * (2 * lax.rem(step, 2) - 1), NZ)

    def at_head(peer):
        return (seq, peer)

    def at_x(peer):
        return (peer * NZ + zi, head)

    def at_z(peer):
        return (xi * NZ + peer, head)

    def every(count, body):
        def step(i, carry):
            body(i)
            return carry

        lax.fori_loop(1, count, step, 0)

    def send(src, dst, send_sem, recv_sem, target):
        return pltpu.make_async_remote_copy(
            src_ref=src, dst_ref=dst, send_sem=send_sem.at[0], recv_sem=recv_sem.at[0],
            device_id=target, device_id_type=MESH,
        )

    def all_of(ref, count, send_sem, recv_sem, target):
        part = ref.at[pl.ds(0, count - 1)]
        return send(part, part, send_sem, recv_sem, target)

    barrier = pltpu.get_barrier_semaphore()

    def greet(peer_of, place):
        def body(step):
            pl.semaphore_signal(
                barrier, inc=1, device_id=place(peer_of(step)), device_id_type=MESH
            )
        return body

    every(nh, greet(head_peer, at_head))
    every(nx, greet(x_peer, at_x))
    every(NZ, greet(z_peer, at_z))
    loads[0].wait()
    maskbuf[head] = jnp.zeros((1, 384), F32)
    maskbuf[head, :, 0:piece] = (mask_ref[...] > 0).astype(F32).reshape(1, piece)
    pl.semaphore_wait(barrier, nh + nx + NZ - 3)

    every(nh, lambda i: send(
        maskbuf.at[head], maskbuf.at[head], m_send, m_recv, at_head(head_peer(i))
    ).start())

    for load in loads[1:5]:
        load.wait()
    lat_key = lk_ref[...]
    lat_value = lv_ref[...]

    def dec_chunk(at, span, carry):
        score = dot(lat_key, pq_ref[span, :], NT) * scale
        e = jnp.exp(score - jnp.max(score, axis=0, keepdims=True))
        p = e * (1.0 / jnp.sum(e, axis=0, keepdims=True))
        dg = dot(lat_value, dg_ref[span, :], NT)
        dd = jnp.sum(p * dg, axis=0, keepdims=True)
        dprob[:, span] = p.astype(BF16)
        dscore[:, span] = (p * (dg - dd)).astype(BF16)
        return carry

    chunks(0, steps, dec_chunk)

    mask_all = all_of(maskbuf, nh, m_send, m_recv, at_head(head_peer(1)))
    mask_all.wait_recv()
    for h in range(nh):
        line = jnp.broadcast_to(maskbuf[h], (128, 384))
        mcol[h * piece:(h + 1) * piece, :] = line.T[:piece, :]

    class Sum:
        def __init__(self, part, rx, summed, rz, full, *sems):
            self.part, self.rx, self.summed, self.rz, self.full = part, rx, summed, rz, full
            self.x_sems, self.z_sems = sems[0:2], sems[2:4]
            self.az_sems, self.ax_sems = sems[4:6], sems[6:8]
            self.whole = [
                all_of(rx, nx, *self.x_sems, at_x(x_peer(1))),
                all_of(rz, NZ, *self.z_sems, at_z(z_peer(1))),
                all_of(full.at[xi], NZ, *self.az_sems, at_z(z_peer(1))),
                all_of(full, nx, *self.ax_sems, at_x(x_peer(1))),
            ]

        def scatter_x(self):
            every(nx, lambda i: send(
                self.part.at[x_peer(i)], self.rx.at[xi], *self.x_sems, at_x(x_peer(i))
            ).start())

        def gathered_x(self):
            self.rx[xi] = self.part[xi]
            self.whole[0].wait_recv()

        def scatter_z(self):
            every(NZ, lambda i: send(
                self.summed.at[z_peer(i)], self.rz.at[zi], *self.z_sems, at_z(z_peer(i))
            ).start())

        def gather_z(self):
            self.rz[zi] = self.summed[zi]
            self.whole[1].wait_recv()
            pieces = [self.rz[i] for i in range(NZ)]
            while len(pieces) > 1:
                pieces = [a + b for a, b in zip(pieces[0::2], pieces[1::2])]
            self.full[xi, zi] = pieces[0]
            every(NZ, lambda i: send(
                self.full.at[xi, zi], self.full.at[xi, zi], *self.az_sems, at_z(z_peer(i))
            ).start())

        def gather_x(self):
            self.whole[2].wait_recv()
            every(nx, lambda i: send(
                self.full.at[xi], self.full.at[xi], *self.ax_sems, at_x(x_peer(i))
            ).start())

        def finish(self):
            self.whole[3].wait_recv()

        def drain(self):
            for copy in self.whole:
                copy.wait_send()

    dec = Sum(
        pdec, rxdec, sumdec, rzdec, fulldec,
        dx_send, dx_recv, dz_send, dz_recv, daz_send, daz_recv, dax_send, dax_recv,
    )
    enc = Sum(
        pq, rxq, sumq, rzq, fullq,
        qx_send, qx_recv, qz_send, qz_recv, qaz_send, qaz_recv, qax_send, qax_recv,
    )
    for load in loads[5:]:
        load.wait()
    lat_query = lq_ref[...]
    enc_grad = eg_ref[...]

    def enc_chunk(at, span, carry):
        bias = (mcol[span, :] - 1.0) * 1e30
        score = dot(pk_ref[span, :], lat_query, NT) * scale
        score = score + jnp.concatenate([bias, bias], axis=1)
        grad = dot(pv_ref[span, :], enc_grad, NT)
        own = jnp.max(score, axis=0, keepdims=True)
        e = jnp.exp(score - own)
        expo[span, :] = e
        edot[span, :] = grad
        own_total = jnp.sum(e, axis=0, keepdims=True)
        own_delta = jnp.sum(e * grad, axis=0, keepdims=True) / own_total
        esums[span, :LAT] = (e * (grad - own_delta)).astype(BF16)
        esums[span, LAT:] = e.astype(BF16)
        tops_ref[at] = own
        totals_ref[at] = own_total
        deltas_ref[at] = own_delta
        return carry

    chunks(0, steps, enc_chunk)
    count = steps * unroll
    tops = [tops_ref[i] for i in range(count)]
    totals = [totals_ref[i] for i in range(count)]
    deltas = [deltas_ref[i] for i in range(count)]
    top = functools.reduce(jnp.maximum, tops)
    shares = [jnp.exp(own - top) for own in tops]
    weights = [w * t for w, t in zip(shares, totals)]
    total = functools.reduce(jnp.add, weights)
    inverse = 1.0 / total
    delta = functools.reduce(jnp.add, [w * d for w, d in zip(weights, deltas)]) * inverse

    def put_stats(ref, slot, lse_rows, delta_rows):
        ref[slot, 0:2, :] = lse_rows
        ref[slot, 2:4, :] = delta_rows

    put_stats(sx, xi, fold(top + jnp.log(total)), fold(delta))
    every(nx, lambda i: send(sx.at[xi], sx.at[xi], sx_send, sx_recv, at_x(x_peer(i))).start())

    def dec_sums(at, span, carry):
        valid = mcol[span, :].astype(BF16)
        key_sum, value_sum = carry
        key_sum = key_sum + dot(dscore[:, span], pq_ref[span, :] * valid, NN)
        value_sum = value_sum + dot(dprob[:, span], dg_ref[span, :] * valid, NN)
        return key_sum, value_sum

    blank = jnp.zeros((LAT, DH), F32)
    key_sum, value_sum = chunks(0, steps, dec_sums, (blank, blank))
    pdec[0:nx // 2] = key_sum.reshape(nx // 2, NZ, 8, 128)
    pdec[nx // 2:nx] = value_sum.reshape(nx // 2, NZ, 8, 128)
    dec.scatter_x()

    sx_all = all_of(sx, nx, sx_send, sx_recv, at_x(x_peer(1)))
    sx_all.wait_recv()
    put_stats(sz, zi, *merge_stats(sx, nx))
    every(NZ, lambda i: send(sz.at[zi], sz.at[zi], sz_send, sz_recv, at_z(z_peer(i))).start())

    def key_sums(at, span, carry):
        a, b = carry
        sums = dot(pk_ref[span, :], esums[span, :], TN)
        w = jnp.exp(tops_ref[at] - top) * inverse
        d = deltas_ref[at]
        a = a + w * (sums[:, :LAT] + (d - delta) * sums[:, LAT:])
        b = b + w * sums[:, LAT:]
        return a, b

    blank = jnp.zeros((DH, LAT), F32)
    a, b = chunks(0, steps, key_sums, (blank, blank))

    def place(i, j):
        at = i * (DH // nx) + (j // 2) * 4
        return slice(at, at + 4), slice((j % 2) * 128, (j % 2) * 128 + 128)

    for i in range(nx):
        for j in range(NZ):
            pq[i, j] = jnp.concatenate([a[place(i, j)], b[place(i, j)]], axis=0)
    enc.scatter_x()

    def dec_packets(at, span, carry):
        grad = dot(dscore[:, span], lat_key, TN) * (mcol[span, :] * scale)
        gpq_ref[span, :] = grad.astype(BF16)
        return carry

    chunks(0, steps, dec_packets)

    dec.gathered_x()
    sumdec[...] = (rxdec[0] + rxdec[1]) + (rxdec[2] + rxdec[3])
    dec.scatter_z()

    sz_all = all_of(sz, NZ, sz_send, sz_recv, at_z(z_peer(1)))
    sz_all.wait_recv()
    lse2, delta2 = merge_stats(sz, NZ)
    enc.gathered_x()
    factors = [jnp.exp(sx[i, 0:2, :] - lse2) for i in range(nx)]
    shifts = [sx[i, 2:4, :] - delta2 for i in range(nx)]
    for j in range(NZ):
        half = slice(j % 2, j % 2 + 1)
        terms = [
            factors[i][half] * (rxq[i, j, 0:4, :] + shifts[i][half] * rxq[i, j, 4:8, :])
            for i in range(nx)
        ]
        sumq[j] = functools.reduce(jnp.add, terms)
    enc.scatter_z()

    lse = jnp.concatenate([lse2[0:1], lse2[1:2]], axis=1)
    delta = jnp.concatenate([delta2[0:1], delta2[1:2]], axis=1)

    def enc_packets(at, span, carry):
        p = expo[span, :] * jnp.exp(tops_ref[at] - lse)
        ds = (p * (edot[span, :] - delta)).astype(BF16)
        gpk_ref[span, :] = (dot(ds, lat_query, NN) * scale).astype(BF16)
        gpv_ref[span, :] = dot(p.astype(BF16), enc_grad, NN).astype(BF16)
        return carry

    chunks(0, 1, enc_packets)
    dec.gather_z()
    chunks(1, steps, enc_packets)
    enc.gather_z()
    dec.gather_x()
    enc.gather_x()
    dec.finish()
    glk_ref[...] = (fulldec[0:nx // 2].reshape(LAT, DH) * scale).astype(BF16)
    glv_ref[...] = fulldec[nx // 2:nx].reshape(LAT, DH)
    enc.finish()
    for i in range(nx):
        for k in range(0, NZ, 4):
            for c in range(2):
                at, lanes = place(i, k + c)
                query_t[at.start:at.start + 8, lanes] = jnp.concatenate(
                    [fullq[i, k + c], fullq[i, k + 2 + c]], axis=0
                )
    glq_ref[...] = (query_t[...].T * scale).astype(BF16)

    mask_all.wait_send()
    sx_all.wait_send()
    sz_all.wait_send()
    dec.drain()
    enc.drain()


def write_out(*refs):
    count = len(refs) // 2
    sems = refs[-1]
    copies = [
        pltpu.make_async_copy(refs[i], refs[count + i], sems.at[i]) for i in range(count)
    ]
    for copy in copies:
        copy.start()
    for copy in copies:
        copy.wait()


def solution(mesh):
    nx = mesh.shape["seq"] // NZ
    nh = mesh.shape["head"]

    def on_device(lq, pk, pv, eg, pq, lk, lv, dg, mask):
        rows = pk.shape[0]
        vmem = pl.BlockSpec(memory_space=pltpu.VMEM)
        hbm = pl.BlockSpec(memory_space=pltpu.HBM)
        lat = jax.ShapeDtypeStruct((LAT, DH), BF16)
        pkt = jax.ShapeDtypeStruct((rows, DH), BF16)
        outs = (lat, pkt, pkt, pkt, lat, jax.ShapeDtypeStruct((LAT, DH), F32))
        args = [
            pltpu.with_memory_space_constraint(x, pltpu.HBM)
            for x in (lq, pk, pv, eg, pq, lk, lv, dg, mask)
        ]

        def reduce_buffers(sent, depth):
            return [
                pltpu.VMEM((nx, NZ, sent, 128), F32),
                pltpu.VMEM((nx, NZ, sent, 128), F32),
                pltpu.VMEM((NZ, depth, 128), F32),
                pltpu.VMEM((NZ, depth, 128), F32),
                pltpu.VMEM((nx, NZ, depth, 128), F32),
            ]

        made = pl.pallas_call(
            functools.partial(kernel, nx, nh, rows),
            out_shape=outs,
            in_specs=[hbm] * len(args),
            out_specs=(vmem,) * len(outs),
            scratch_shapes=[pltpu.VMEM(x.shape, x.dtype) for x in args]
            + [
                pltpu.VMEM((nh, 1, 384), F32),
                pltpu.VMEM((rows, 128), F32),
                pltpu.VMEM((rows, LAT), F32),
                pltpu.VMEM((rows, LAT), F32),
                pltpu.VMEM((rows, 2 * LAT), BF16),
                pltpu.VMEM((LAT, rows), BF16),
                pltpu.VMEM((LAT, rows), BF16),
                pltpu.VMEM((DH, LAT), F32),
                pltpu.VMEM((6, 1, LAT), F32),
                pltpu.VMEM((6, 1, LAT), F32),
                pltpu.VMEM((6, 1, LAT), F32),
                pltpu.VMEM((nx, 4, 128), F32),
                pltpu.VMEM((NZ, 4, 128), F32),
            ]
            + reduce_buffers(8, 8)
            + reduce_buffers(8, 4)
            + [pltpu.SemaphoreType.DMA((len(args),))]
            + [pltpu.SemaphoreType.DMA((1,))] * 22,
            compiler_params=pltpu.CompilerParams(
                collective_id=0, has_side_effects=True, vmem_limit_bytes=48 * 2**20
            ),
            name="perceiver_backward",
        )(*args)
        return pl.pallas_call(
            write_out,
            out_shape=outs,
            in_specs=[vmem] * len(outs),
            out_specs=(hbm,) * len(outs),
            scratch_shapes=[pltpu.SemaphoreType.DMA((len(outs),))],
            compiler_params=pltpu.CompilerParams(vmem_limit_bytes=2**20),
            name="write_out",
        )(*[pltpu.with_memory_space_constraint(x, pltpu.VMEM) for x in made])

    return jax.shard_map(
        on_device,
        mesh=mesh,
        in_specs=(
            P(None, "head"),
            P("seq", "head"),
            P("seq", "head"),
            P(None, "head"),
            P("seq", "head"),
            P(None, "head"),
            P(None, "head"),
            P("seq", "head"),
            P(("seq", "head")),
        ),
        out_specs=(
            P(None, "head"),
            P("seq", "head"),
            P("seq", "head"),
            P("seq", "head"),
            P(None, "head"),
            P(None, "head"),
        ),
        check_vma=False,
    )
```

```python
import functools
import math

import jax
import jax.numpy as jnp
from jax import lax
from jax.experimental import pallas as pl
from jax.experimental.pallas import tpu as pltpu
from jax.sharding import PartitionSpec as P

DH = 128
LAT = 256
NZ = 16
NL = 4
NH = NZ // NL
MESH = pl.DeviceIdType.MESH
F32 = jnp.float32
BF16 = jnp.bfloat16
NT = (((1,), (1,)), ((), ()))
NN = (((1,), (0,)), ((), ()))
TN = (((0,), (0,)), ((), ()))


def dot(a, b, dims):
    return lax.dot_general(a, b, dims, preferred_element_type=F32)


def merge_stats(ref, count):
    lses = [ref[i, 0:2, :] for i in range(count)]
    top = functools.reduce(jnp.maximum, lses)
    weights = [jnp.exp(lse - top) for lse in lses]
    total = functools.reduce(jnp.add, weights)
    mixed = functools.reduce(jnp.add, [w * ref[i, 2:4, :] for i, w in enumerate(weights)])
    return top + jnp.log(total), mixed / total


def tree_sum(pieces):
    while len(pieces) > 1:
        pieces = [a + b for a, b in zip(pieces[0::2], pieces[1::2])]
    return pieces[0]


def fold(line):
    return jnp.concatenate([line[:, :128], line[:, 128:]], axis=0)


def kernel(
    nx, nh, rows,
    lq_hbm, pk_hbm, pv_hbm, eg_hbm, pq_hbm, lk_hbm, lv_hbm, dg_hbm, mask_hbm,
    glq_ref, gpk_ref, gpv_ref, gpq_ref, glk_ref, glv_ref,
    lq_ref, pk_ref, pv_ref, eg_ref, pq_ref, lk_ref, lv_ref, dg_ref, mask_ref,
    maskbuf, mcol, expo, edot, esums, dprob, dscore, query_t,
    sx, sl, sh, *rest,
):
    pdec, rxdec, sumdec, rldec, midec, rhdec, fulldec = rest[0:7]
    pq, rxq, sumq, rlq, midq, rhq, fullq = rest[7:14]
    in_sems = rest[14]
    m_sems, sx_sems, sl_sems, sh_sems, *sum_sems = [
        tuple(rest[i:i + 2]) for i in range(15, len(rest), 2)
    ]
    scale = 1.0 / math.sqrt(DH)
    piece = rows // nh
    size = 384
    spans = [slice(at, at + size) for at in range(0, rows, size)]
    seq = lax.axis_index("seq")
    head = lax.axis_index("head")
    xi = seq // NZ
    zi = lax.rem(seq, NZ)
    li = lax.rem(zi, NL)
    hi = zi // NL

    loads = [
        pltpu.make_async_copy(src, dst, in_sems.at[i])
        for i, (src, dst) in enumerate(
            (
                (mask_hbm, mask_ref),
                (pq_hbm, pq_ref),
                (lk_hbm, lk_ref),
                (dg_hbm, dg_ref),
                (lv_hbm, lv_ref),
                (pk_hbm, pk_ref),
                (lq_hbm, lq_ref),
                (pv_hbm, pv_ref),
                (eg_hbm, eg_ref),
            )
        )
    ]
    for load in loads:
        load.start()

    def head_peer(step):
        return lax.rem(head + step, nh)

    def x_peer(step):
        return lax.rem(xi + step, nx)

    def l_peer(step):
        return lax.rem(li + step, NL)

    def h_peer(step):
        return lax.rem(hi + step, NH)

    def at_head(peer):
        return (seq, peer)

    def at_x(peer):
        return (peer * NZ + zi, head)

    def at_l(peer):
        return (xi * NZ + hi * NL + peer, head)

    def at_h(peer):
        return (xi * NZ + peer * NL + li, head)

    def every(count, body):
        def step(i, carry):
            body(i)
            return carry

        lax.fori_loop(1, count, step, 0)

    def send(src, dst, send_sem, recv_sem, target):
        return pltpu.make_async_remote_copy(
            src_ref=src, dst_ref=dst, send_sem=send_sem.at[0], recv_sem=recv_sem.at[0],
            device_id=target, device_id_type=MESH,
        )

    def all_of(ref, count, send_sem, recv_sem, target):
        part = ref.at[pl.ds(0, count - 1)]
        return send(part, part, send_sem, recv_sem, target)

    barrier = pltpu.get_barrier_semaphore()

    def greet(peer_of, place):
        def body(step):
            pl.semaphore_signal(
                barrier, inc=1, device_id=place(peer_of(step)), device_id_type=MESH
            )
        return body

    every(nh, greet(head_peer, at_head))
    every(nx, greet(x_peer, at_x))
    every(NL, greet(l_peer, at_l))
    every(NH, greet(h_peer, at_h))
    loads[0].wait()
    maskbuf[head] = jnp.zeros((1, 384), F32)
    maskbuf[head, :, 0:piece] = (mask_ref[...] > 0).astype(F32).reshape(1, piece)
    def start_masks():
        pl.semaphore_wait(barrier, nh + nx + NL + NH - 4)
        every(nh, lambda i: send(
            maskbuf.at[head], maskbuf.at[head], *m_sems, at_head(head_peer(i))
        ).start())

    for load in loads[1:5]:
        load.wait()
    lat_key = lk_ref[...]
    lat_value = lv_ref[...]
    for at, span in enumerate(spans):
        if at == len(spans) // 2:
            start_masks()
        score = dot(lat_key, pq_ref[span, :], NT) * scale
        e = jnp.exp(score - jnp.max(score, axis=0, keepdims=True))
        p = e * (1.0 / jnp.sum(e, axis=0, keepdims=True))
        dg = dot(lat_value, dg_ref[span, :], NT)
        dd = jnp.sum(p * dg, axis=0, keepdims=True)
        dprob[:, span] = p.astype(BF16)
        dscore[:, span] = (p * (dg - dd)).astype(BF16)

    mask_all = all_of(maskbuf, nh, *m_sems, at_head(head_peer(1)))
    mask_all.wait_recv()
    for h in range(nh):
        line = jnp.broadcast_to(maskbuf[h], (128, 384))
        mcol[h * piece:(h + 1) * piece, :] = line.T[:piece, :]

    class Sum:
        def __init__(self, part, rx, summed, rl, middle, rh, full, x, l, h, ah, al, ax):
            self.part, self.rx, self.summed, self.rl = part, rx, summed, rl
            self.middle, self.rh, self.full = middle, rh, full
            self.x, self.l, self.h, self.ah, self.al, self.ax = x, l, h, ah, al, ax
            self.own = full.at[xi, li]
            self.whole = [
                all_of(rx, nx, *x, at_x(x_peer(1))),
                all_of(rl, NL, *l, at_l(l_peer(1))),
                all_of(rh, NH, *h, at_h(h_peer(1))),
                all_of(self.own, NH, *ah, at_h(h_peer(1))),
                all_of(full.at[xi], NL, *al, at_l(l_peer(1))),
                all_of(full, nx, *ax, at_x(x_peer(1))),
            ]

        def scatter_x(self):
            every(nx, lambda i: send(
                self.part.at[x_peer(i)], self.rx.at[xi], *self.x, at_x(x_peer(i))
            ).start())

        def gathered_x(self):
            self.rx[xi] = self.part[xi]
            self.whole[0].wait_recv()

        def scatter_l(self):
            every(NL, lambda i: send(
                self.summed.at[l_peer(i)], self.rl.at[li], *self.l, at_l(l_peer(i))
            ).start())

        def scatter_h(self):
            self.rl[li] = self.summed[li]
            self.whole[1].wait_recv()
            self.middle[...] = tree_sum([self.rl[i] for i in range(NL)])
            every(NH, lambda i: send(
                self.middle.at[h_peer(i)], self.rh.at[hi], *self.h, at_h(h_peer(i))
            ).start())

        def gather_h(self):
            self.rh[hi] = self.middle[hi]
            self.whole[2].wait_recv()
            self.full[xi, li, hi] = tree_sum([self.rh[i] for i in range(NH)])
            every(NH, lambda i: send(
                self.own.at[hi], self.own.at[hi], *self.ah, at_h(h_peer(i))
            ).start())

        def gather_l(self):
            self.whole[3].wait_recv()
            every(NL, lambda i: send(self.own, self.own, *self.al, at_l(l_peer(i))).start())

        def gather_x(self):
            self.whole[4].wait_recv()
            every(nx, lambda i: send(
                self.full.at[xi], self.full.at[xi], *self.ax, at_x(x_peer(i))
            ).start())

        def finish(self):
            self.whole[5].wait_recv()

        def drain(self):
            for copy in self.whole:
                copy.wait_send()

    dec = Sum(pdec, rxdec, sumdec, rldec, midec, rhdec, fulldec, *sum_sems[0:6])
    enc = Sum(pq, rxq, sumq, rlq, midq, rhq, fullq, *sum_sems[6:12])

    for load in loads[5:]:
        load.wait()
    lat_query = lq_ref[...]
    enc_grad = eg_ref[...]
    tops, totals, deltas = [], [], []
    for span in spans:
        bias = (mcol[span, :] - 1.0) * 1e30
        score = dot(pk_ref[span, :], lat_query, NT) * scale
        score = score + jnp.concatenate([bias, bias], axis=1)
        grad = dot(pv_ref[span, :], enc_grad, NT)
        own = jnp.max(score, axis=0, keepdims=True)
        e = jnp.exp(score - own)
        expo[span, :] = e
        edot[span, :] = grad
        own_total = jnp.sum(e, axis=0, keepdims=True)
        own_delta = jnp.sum(e * grad, axis=0, keepdims=True) / own_total
        esums[span, :LAT] = (e * (grad - own_delta)).astype(BF16)
        esums[span, LAT:] = e.astype(BF16)
        tops.append(own)
        totals.append(own_total)
        deltas.append(own_delta)
    top = functools.reduce(jnp.maximum, tops)
    shares = [jnp.exp(own - top) for own in tops]
    weights = [w * t for w, t in zip(shares, totals)]
    total = functools.reduce(jnp.add, weights)
    inverse = 1.0 / total
    delta = functools.reduce(jnp.add, [w * d for w, d in zip(weights, deltas)]) * inverse

    def put_stats(ref, slot, lse_rows, delta_rows):
        ref[slot, 0:2, :] = lse_rows
        ref[slot, 2:4, :] = delta_rows

    put_stats(sx, xi, fold(top + jnp.log(total)), fold(delta))
    every(nx, lambda i: send(sx.at[xi], sx.at[xi], *sx_sems, at_x(x_peer(i))).start())

    key_sum = jnp.zeros((LAT, DH), F32)
    value_sum = jnp.zeros((LAT, DH), F32)
    for span in spans:
        valid = mcol[span, :].astype(BF16)
        key_sum = key_sum + dot(dscore[:, span], pq_ref[span, :] * valid, NN)
        value_sum = value_sum + dot(dprob[:, span], dg_ref[span, :] * valid, NN)
    pdec[0:nx // 2] = key_sum.reshape(nx // 2, NL, NH, 8, 128)
    pdec[nx // 2:nx] = value_sum.reshape(nx // 2, NL, NH, 8, 128)
    dec.scatter_x()

    sx_all = all_of(sx, nx, *sx_sems, at_x(x_peer(1)))
    sx_all.wait_recv()
    put_stats(sl, li, *merge_stats(sx, nx))
    every(NL, lambda i: send(sl.at[li], sl.at[li], *sl_sems, at_l(l_peer(i))).start())

    a = jnp.zeros((DH, LAT), F32)
    b = jnp.zeros((DH, LAT), F32)
    for span, w, d in zip(spans, shares, deltas):
        sums = dot(pk_ref[span, :], esums[span, :], TN)
        w = w * inverse
        a = a + w * (sums[:, :LAT] + (d - delta) * sums[:, LAT:])
        b = b + w * sums[:, LAT:]

    def place(i, j):
        at = i * (DH // nx) + (j // 2) * 4
        return slice(at, at + 4), slice((j % 2) * 128, (j % 2) * 128 + 128)

    for i in range(nx):
        for j in range(NZ):
            pq[i, j // NH, j % NH] = jnp.concatenate([a[place(i, j)], b[place(i, j)]], axis=0)
    enc.scatter_x()

    sl_all = all_of(sl, NL, *sl_sems, at_l(l_peer(1)))
    sl_all.wait_recv()
    put_stats(sh, hi, *merge_stats(sl, NL))
    every(NH, lambda i: send(sh.at[hi], sh.at[hi], *sh_sems, at_h(h_peer(i))).start())

    dec.gathered_x()
    sumdec[...] = tree_sum([rxdec[i] for i in range(nx)])
    dec.scatter_l()

    for span in spans:
        grad = dot(dscore[:, span], lat_key, TN) * (mcol[span, :] * scale)
        gpq_ref[span, :] = grad.astype(BF16)

    sh_all = all_of(sh, NH, *sh_sems, at_h(h_peer(1)))
    sh_all.wait_recv()
    lse2, delta2 = merge_stats(sh, NH)
    enc.gathered_x()
    factors = [jnp.exp(sx[i, 0:2, :] - lse2) for i in range(nx)]
    shifts = [sx[i, 2:4, :] - delta2 for i in range(nx)]
    for j in range(NZ):
        half = slice(j % 2, j % 2 + 1)
        terms = [
            factors[i][half] * (rxq[i, j // NH, j % NH, 0:4, :] + shifts[i][half] * rxq[i, j // NH, j % NH, 4:8, :])
            for i in range(nx)
        ]
        sumq[j // NH, j % NH] = functools.reduce(jnp.add, terms)
    enc.scatter_l()

    lse = jnp.concatenate([lse2[0:1], lse2[1:2]], axis=1)
    delta = jnp.concatenate([delta2[0:1], delta2[1:2]], axis=1)

    def enc_packets(first, last):
        for span, own in zip(spans[first:last], tops[first:last]):
            p = expo[span, :] * jnp.exp(own - lse)
            ds = (p * (edot[span, :] - delta)).astype(BF16)
            gpk_ref[span, :] = (dot(ds, lat_query, NN) * scale).astype(BF16)
            gpv_ref[span, :] = dot(p.astype(BF16), enc_grad, NN).astype(BF16)

    enc_packets(0, 2)
    dec.scatter_h()
    enc_packets(2, 3)
    enc.scatter_h()
    enc_packets(3, 4)
    dec.gather_h()
    enc.gather_h()
    enc_packets(4, len(spans))
    dec.gather_l()
    enc.gather_l()
    dec.gather_x()
    enc.gather_x()
    dec.finish()
    glk_ref[...] = (fulldec[0:nx // 2].reshape(LAT, DH) * scale).astype(BF16)
    glv_ref[...] = fulldec[nx // 2:nx].reshape(LAT, DH)
    enc.finish()
    for i in range(nx):
        for k in range(0, NZ, 4):
            for c in range(2):
                at, lanes = place(i, k + c)
                query_t[at.start:at.start + 8, lanes] = jnp.concatenate(
                    [fullq[i, j // NH, j % NH] for j in (k + c, k + 2 + c)], axis=0
                )
    glq_ref[...] = (query_t[...].T * scale).astype(BF16)

    mask_all.wait_send()
    sx_all.wait_send()
    sl_all.wait_send()
    sh_all.wait_send()
    dec.drain()
    enc.drain()


def write_out(*refs):
    count = len(refs) // 2
    sems = refs[-1]
    copies = [
        pltpu.make_async_copy(refs[i], refs[count + i], sems.at[i]) for i in range(count)
    ]
    for copy in copies:
        copy.start()
    for copy in copies:
        copy.wait()


def solution(mesh):
    nx = mesh.shape["seq"] // NZ
    nh = mesh.shape["head"]

    def on_device(lq, pk, pv, eg, pq, lk, lv, dg, mask):
        rows = pk.shape[0]
        vmem = pl.BlockSpec(memory_space=pltpu.VMEM)
        hbm = pl.BlockSpec(memory_space=pltpu.HBM)
        lat = jax.ShapeDtypeStruct((LAT, DH), BF16)
        pkt = jax.ShapeDtypeStruct((rows, DH), BF16)
        outs = (lat, pkt, pkt, pkt, lat, jax.ShapeDtypeStruct((LAT, DH), F32))
        args = [
            pltpu.with_memory_space_constraint(x, pltpu.HBM)
            for x in (lq, pk, pv, eg, pq, lk, lv, dg, mask)
        ]

        def reduce_buffers(sent, depth):
            return [
                pltpu.VMEM((nx, NL, NH, sent, 128), F32),
                pltpu.VMEM((nx, NL, NH, sent, 128), F32),
                pltpu.VMEM((NL, NH, depth, 128), F32),
                pltpu.VMEM((NL, NH, depth, 128), F32),
                pltpu.VMEM((NH, depth, 128), F32),
                pltpu.VMEM((NH, depth, 128), F32),
                pltpu.VMEM((nx, NL, NH, depth, 128), F32),
            ]

        made = pl.pallas_call(
            functools.partial(kernel, nx, nh, rows),
            out_shape=outs,
            in_specs=[hbm] * len(args),
            out_specs=(vmem,) * len(outs),
            scratch_shapes=[pltpu.VMEM(x.shape, x.dtype) for x in args]
            + [
                pltpu.VMEM((nh, 1, 384), F32),
                pltpu.VMEM((rows, 128), F32),
                pltpu.VMEM((rows, LAT), F32),
                pltpu.VMEM((rows, LAT), F32),
                pltpu.VMEM((rows, 2 * LAT), BF16),
                pltpu.VMEM((LAT, rows), BF16),
                pltpu.VMEM((LAT, rows), BF16),
                pltpu.VMEM((DH, LAT), F32),
                pltpu.VMEM((nx, 4, 128), F32),
                pltpu.VMEM((NL, 4, 128), F32),
                pltpu.VMEM((NH, 4, 128), F32),
            ]
            + reduce_buffers(8, 8)
            + reduce_buffers(8, 4)
            + [pltpu.SemaphoreType.DMA((len(args),))]
            + [pltpu.SemaphoreType.DMA((1,))] * 32,
            compiler_params=pltpu.CompilerParams(
                collective_id=0, has_side_effects=True, vmem_limit_bytes=48 * 2**20
            ),
            name="perceiver_backward",
        )(*args)
        return pl.pallas_call(
            write_out,
            out_shape=outs,
            in_specs=[vmem] * len(outs),
            out_specs=(hbm,) * len(outs),
            scratch_shapes=[pltpu.SemaphoreType.DMA((len(outs),))],
            compiler_params=pltpu.CompilerParams(vmem_limit_bytes=2**20),
            name="write_out",
        )(*[pltpu.with_memory_space_constraint(x, pltpu.VMEM) for x in made])

    return jax.shard_map(
        on_device,
        mesh=mesh,
        in_specs=(
            P(None, "head"),
            P("seq", "head"),
            P("seq", "head"),
            P(None, "head"),
            P("seq", "head"),
            P(None, "head"),
            P(None, "head"),
            P("seq", "head"),
            P(("seq", "head")),
        ),
        out_specs=(
            P(None, "head"),
            P("seq", "head"),
            P("seq", "head"),
            P("seq", "head"),
            P(None, "head"),
            P(None, "head"),
        ),
        check_vma=False,
    )
```

```python
import functools
import math

import jax
import jax.numpy as jnp
from jax import lax
from jax.experimental import pallas as pl
from jax.experimental.pallas import tpu as pltpu
from jax.sharding import PartitionSpec as P

DH = 128
LAT = 256
Z = 16
NZ = 8
MESH = pl.DeviceIdType.MESH
F32 = jnp.float32
BF16 = jnp.bfloat16
NT = (((1,), (1,)), ((), ()))
NN = (((1,), (0,)), ((), ()))
TN = (((0,), (0,)), ((), ()))


def dot(a, b, dims):
    return lax.dot_general(a, b, dims, preferred_element_type=F32)


def merge_stats(ref, count):
    lses = [ref[i, 0:2, :] for i in range(count)]
    top = functools.reduce(jnp.maximum, lses)
    weights = [jnp.exp(lse - top) for lse in lses]
    total = functools.reduce(jnp.add, weights)
    mixed = functools.reduce(jnp.add, [w * ref[i, 2:4, :] for i, w in enumerate(weights)])
    return top + jnp.log(total), mixed / total


def tree_sum(pieces):
    while len(pieces) > 1:
        pieces = [a + b for a, b in zip(pieces[0::2], pieces[1::2])]
    return pieces[0]


def fold(line):
    return jnp.concatenate([line[:, :128], line[:, 128:]], axis=0)


def kernel(
    nx, nh, rows,
    lq_hbm, pk_hbm, pv_hbm, eg_hbm, pq_hbm, lk_hbm, lv_hbm, dg_hbm, mask_hbm,
    glq_ref, gpk_ref, gpv_ref, gpq_ref, glk_ref, glv_ref,
    lq_ref, pk_ref, pv_ref, eg_ref, pq_ref, lk_ref, lv_ref, dg_ref, mask_ref,
    maskbuf, mcol, expo, edot, esums, dprob, dscore, query_t,
    sx, sz, pdec, rxdec, sumdec, rzdec, fulldec, pq, rxq, sumq, rzq, fullq,
    in_sems,
    m_send, m_recv, sx_send, sx_recv, sz_send, sz_recv,
    dx_send, dx_recv, dz_send, dz_recv, daz_send, daz_recv, dax_send, dax_recv,
    qx_send, qx_recv, qz_send, qz_recv, qaz_send, qaz_recv, qax_send, qax_recv,
):
    scale = 1.0 / math.sqrt(DH)
    piece = rows // nh
    size = 384
    spans = [slice(at, at + size) for at in range(0, rows, size)]
    seq = lax.axis_index("seq")
    head = lax.axis_index("head")
    low = Z // NZ
    xi = (seq // Z) * low + lax.rem(seq, low)
    zi = lax.rem(seq, Z) // low

    loads = [
        pltpu.make_async_copy(src, dst, in_sems.at[i])
        for i, (src, dst) in enumerate(
            (
                (mask_hbm, mask_ref),
                (pq_hbm, pq_ref),
                (lk_hbm, lk_ref),
                (dg_hbm, dg_ref),
                (lv_hbm, lv_ref),
                (pk_hbm, pk_ref),
                (lq_hbm, lq_ref),
                (pv_hbm, pv_ref),
                (eg_hbm, eg_ref),
            )
        )
    ]
    for load in loads:
        load.start()

    def head_peer(step):
        return lax.rem(head + step, nh)

    def x_peer(step):
        return lax.rem(xi + step, nx)

    def z_peer(step):
        return lax.rem(zi + NZ // 2 + (step // 2) * (2 * lax.rem(step, 2) - 1), NZ)

    def at_head(peer):
        return (seq, peer)

    def at_x(peer):
        return ((peer // low) * Z + zi * low + lax.rem(peer, low), head)

    def at_z(peer):
        return ((xi // low) * Z + peer * low + lax.rem(xi, low), head)

    def every(count, body):
        def step(i, carry):
            body(i)
            return carry

        lax.fori_loop(1, count, step, 0)

    def send(src, dst, send_sem, recv_sem, target):
        return pltpu.make_async_remote_copy(
            src_ref=src, dst_ref=dst, send_sem=send_sem.at[0], recv_sem=recv_sem.at[0],
            device_id=target, device_id_type=MESH,
        )

    def all_of(ref, count, send_sem, recv_sem, target):
        part = ref.at[pl.ds(0, count - 1)]
        return send(part, part, send_sem, recv_sem, target)

    barrier = pltpu.get_barrier_semaphore()

    def greet(peer_of, place):
        def body(step):
            pl.semaphore_signal(
                barrier, inc=1, device_id=place(peer_of(step)), device_id_type=MESH
            )
        return body

    every(nh, greet(head_peer, at_head))
    every(nx, greet(x_peer, at_x))
    every(NZ, greet(z_peer, at_z))
    loads[0].wait()
    maskbuf[head] = jnp.zeros((1, 384), F32)
    maskbuf[head, :, 0:piece] = (mask_ref[...] > 0).astype(F32).reshape(1, piece)
    pl.semaphore_wait(barrier, nh + nx + NZ - 3)

    every(nh, lambda i: send(
        maskbuf.at[head], maskbuf.at[head], m_send, m_recv, at_head(head_peer(i))
    ).start())

    for load in loads[1:5]:
        load.wait()
    lat_key = lk_ref[...]
    lat_value = lv_ref[...]
    for span in spans:
        score = dot(lat_key, pq_ref[span, :], NT) * scale
        e = jnp.exp(score - jnp.max(score, axis=0, keepdims=True))
        p = e * (1.0 / jnp.sum(e, axis=0, keepdims=True))
        dg = dot(lat_value, dg_ref[span, :], NT)
        dd = jnp.sum(p * dg, axis=0, keepdims=True)
        dprob[:, span] = p.astype(BF16)
        dscore[:, span] = (p * (dg - dd)).astype(BF16)

    mask_all = all_of(maskbuf, nh, m_send, m_recv, at_head(head_peer(1)))
    mask_all.wait_recv()
    for h in range(nh):
        line = jnp.broadcast_to(maskbuf[h], (128, 384))
        mcol[h * piece:(h + 1) * piece, :] = line.T[:piece, :]

    class Sum:
        def __init__(self, part, rx, summed, rz, full, *sems):
            self.part, self.rx, self.summed, self.rz, self.full = part, rx, summed, rz, full
            self.x_sems, self.z_sems = sems[0:2], sems[2:4]
            self.az_sems, self.ax_sems = sems[4:6], sems[6:8]
            self.whole = [
                all_of(rx, nx, *self.x_sems, at_x(x_peer(1))),
                all_of(rz, NZ, *self.z_sems, at_z(z_peer(1))),
                all_of(full.at[xi], NZ, *self.az_sems, at_z(z_peer(1))),
                all_of(full, nx, *self.ax_sems, at_x(x_peer(1))),
            ]

        def scatter_x(self):
            every(nx, lambda i: send(
                self.part.at[x_peer(i)], self.rx.at[xi], *self.x_sems, at_x(x_peer(i))
            ).start())

        def gathered_x(self):
            self.rx[xi] = self.part[xi]
            self.whole[0].wait_recv()

        def scatter_z(self):
            every(NZ, lambda i: send(
                self.summed.at[z_peer(i)], self.rz.at[zi], *self.z_sems, at_z(z_peer(i))
            ).start())

        def gather_z(self):
            self.rz[zi] = self.summed[zi]
            self.whole[1].wait_recv()
            self.full[xi, zi] = tree_sum([self.rz[i] for i in range(NZ)])
            every(NZ, lambda i: send(
                self.full.at[xi, zi], self.full.at[xi, zi], *self.az_sems, at_z(z_peer(i))
            ).start())

        def gather_x(self):
            self.whole[2].wait_recv()
            every(nx, lambda i: send(
                self.full.at[xi], self.full.at[xi], *self.ax_sems, at_x(x_peer(i))
            ).start())

        def finish(self):
            self.whole[3].wait_recv()

        def drain(self):
            for copy in self.whole:
                copy.wait_send()

    dec = Sum(
        pdec, rxdec, sumdec, rzdec, fulldec,
        dx_send, dx_recv, dz_send, dz_recv, daz_send, daz_recv, dax_send, dax_recv,
    )
    enc = Sum(
        pq, rxq, sumq, rzq, fullq,
        qx_send, qx_recv, qz_send, qz_recv, qaz_send, qaz_recv, qax_send, qax_recv,
    )
    for load in loads[5:]:
        load.wait()
    lat_query = lq_ref[...]
    enc_grad = eg_ref[...]
    tops, totals, deltas = [], [], []
    for span in spans:
        bias = (mcol[span, :] - 1.0) * 1e30
        score = dot(pk_ref[span, :], lat_query, NT) * scale
        score = score + jnp.concatenate([bias, bias], axis=1)
        grad = dot(pv_ref[span, :], enc_grad, NT)
        own = jnp.max(score, axis=0, keepdims=True)
        e = jnp.exp(score - own)
        expo[span, :] = e
        edot[span, :] = grad
        own_total = jnp.sum(e, axis=0, keepdims=True)
        own_delta = jnp.sum(e * grad, axis=0, keepdims=True) / own_total
        esums[span, :LAT] = (e * (grad - own_delta)).astype(BF16)
        esums[span, LAT:] = e.astype(BF16)
        tops.append(own)
        totals.append(own_total)
        deltas.append(own_delta)
    top = functools.reduce(jnp.maximum, tops)
    shares = [jnp.exp(own - top) for own in tops]
    weights = [w * t for w, t in zip(shares, totals)]
    total = functools.reduce(jnp.add, weights)
    inverse = 1.0 / total
    delta = functools.reduce(jnp.add, [w * d for w, d in zip(weights, deltas)]) * inverse

    def put_stats(ref, slot, lse_rows, delta_rows):
        ref[slot, 0:2, :] = lse_rows
        ref[slot, 2:4, :] = delta_rows

    put_stats(sx, xi, fold(top + jnp.log(total)), fold(delta))
    every(nx, lambda i: send(sx.at[xi], sx.at[xi], sx_send, sx_recv, at_x(x_peer(i))).start())

    a = jnp.zeros((DH, LAT), F32)
    b = jnp.zeros((DH, LAT), F32)
    for span, w, d in zip(spans, shares, deltas):
        sums = dot(pk_ref[span, :], esums[span, :], TN)
        w = w * inverse
        a = a + w * (sums[:, :LAT] + (d - delta) * sums[:, LAT:])
        b = b + w * sums[:, LAT:]

    def place(i, j):
        at = i * (DH // nx) + (j // 2) * 4
        return slice(at, at + 4), slice((j % 2) * 128, (j % 2) * 128 + 128)

    for i in range(nx):
        for j in range(NZ):
            pq[i, j] = jnp.concatenate([a[place(i, j)], b[place(i, j)]], axis=0)
    enc.scatter_x()

    key_sum = jnp.zeros((LAT, DH), F32)
    value_sum = jnp.zeros((LAT, DH), F32)
    for span in spans:
        valid = mcol[span, :].astype(BF16)
        key_sum = key_sum + dot(dscore[:, span], pq_ref[span, :] * valid, NN)
        value_sum = value_sum + dot(dprob[:, span], dg_ref[span, :] * valid, NN)
    pdec[0:nx // 2] = key_sum.reshape(nx // 2, NZ, 8, 128)
    pdec[nx // 2:nx] = value_sum.reshape(nx // 2, NZ, 8, 128)
    dec.scatter_x()

    sx_all = all_of(sx, nx, sx_send, sx_recv, at_x(x_peer(1)))
    sx_all.wait_recv()
    put_stats(sz, zi, *merge_stats(sx, nx))
    every(NZ, lambda i: send(sz.at[zi], sz.at[zi], sz_send, sz_recv, at_z(z_peer(i))).start())

    for span in spans:
        grad = dot(dscore[:, span], lat_key, TN) * (mcol[span, :] * scale)
        gpq_ref[span, :] = grad.astype(BF16)

    sz_all = all_of(sz, NZ, sz_send, sz_recv, at_z(z_peer(1)))
    sz_all.wait_recv()
    lse2, delta2 = merge_stats(sz, NZ)
    enc.gathered_x()
    factors = [jnp.exp(sx[i, 0:2, :] - lse2) for i in range(nx)]
    shifts = [sx[i, 2:4, :] - delta2 for i in range(nx)]
    for j in range(NZ):
        half = slice(j % 2, j % 2 + 1)
        terms = [
            factors[i][half] * (rxq[i, j, 0:4, :] + shifts[i][half] * rxq[i, j, 4:8, :])
            for i in range(nx)
        ]
        sumq[j] = functools.reduce(jnp.add, terms)
    enc.scatter_z()

    dec.gathered_x()
    sumdec[...] = tree_sum([rxdec[i] for i in range(nx)])
    dec.scatter_z()

    lse = jnp.concatenate([lse2[0:1], lse2[1:2]], axis=1)
    delta = jnp.concatenate([delta2[0:1], delta2[1:2]], axis=1)

    def enc_packets(first, last):
        for span, own in zip(spans[first:last], tops[first:last]):
            p = expo[span, :] * jnp.exp(own - lse)
            ds = (p * (edot[span, :] - delta)).astype(BF16)
            gpk_ref[span, :] = (dot(ds, lat_query, NN) * scale).astype(BF16)
            gpv_ref[span, :] = dot(p.astype(BF16), enc_grad, NN).astype(BF16)

    enc_packets(0, 3)
    enc.gather_z()
    enc_packets(3, 4)
    dec.gather_z()
    enc_packets(4, len(spans))
    enc.gather_x()
    dec.gather_x()
    enc.finish()
    for i in range(nx):
        for k in range(0, NZ, 4):
            for c in range(2):
                at, lanes = place(i, k + c)
                query_t[at.start:at.start + 8, lanes] = jnp.concatenate(
                    [fullq[i, k + c], fullq[i, k + 2 + c]], axis=0
                )
    glq_ref[...] = (query_t[...].T * scale).astype(BF16)

    dec.finish()
    glk_ref[...] = (fulldec[0:nx // 2].reshape(LAT, DH) * scale).astype(BF16)
    glv_ref[...] = fulldec[nx // 2:nx].reshape(LAT, DH)

    mask_all.wait_send()
    sx_all.wait_send()
    sz_all.wait_send()
    dec.drain()
    enc.drain()


def write_out(*refs):
    count = len(refs) // 2
    sems = refs[-1]
    copies = [
        pltpu.make_async_copy(refs[i], refs[count + i], sems.at[i]) for i in range(count)
    ]
    for copy in copies:
        copy.start()
    for copy in copies:
        copy.wait()


def solution(mesh):
    nx = mesh.shape["seq"] // NZ
    nh = mesh.shape["head"]

    def on_device(lq, pk, pv, eg, pq, lk, lv, dg, mask):
        rows = pk.shape[0]
        vmem = pl.BlockSpec(memory_space=pltpu.VMEM)
        hbm = pl.BlockSpec(memory_space=pltpu.HBM)
        lat = jax.ShapeDtypeStruct((LAT, DH), BF16)
        pkt = jax.ShapeDtypeStruct((rows, DH), BF16)
        outs = (lat, pkt, pkt, pkt, lat, jax.ShapeDtypeStruct((LAT, DH), F32))
        args = [
            pltpu.with_memory_space_constraint(x, pltpu.HBM)
            for x in (lq, pk, pv, eg, pq, lk, lv, dg, mask)
        ]

        def reduce_buffers(sent, depth):
            return [
                pltpu.VMEM((nx, NZ, sent, 128), F32),
                pltpu.VMEM((nx, NZ, sent, 128), F32),
                pltpu.VMEM((NZ, depth, 128), F32),
                pltpu.VMEM((NZ, depth, 128), F32),
                pltpu.VMEM((nx, NZ, depth, 128), F32),
            ]

        made = pl.pallas_call(
            functools.partial(kernel, nx, nh, rows),
            out_shape=outs,
            in_specs=[hbm] * len(args),
            out_specs=(vmem,) * len(outs),
            scratch_shapes=[pltpu.VMEM(x.shape, x.dtype) for x in args]
            + [
                pltpu.VMEM((nh, 1, 384), F32),
                pltpu.VMEM((rows, 128), F32),
                pltpu.VMEM((rows, LAT), F32),
                pltpu.VMEM((rows, LAT), F32),
                pltpu.VMEM((rows, 2 * LAT), BF16),
                pltpu.VMEM((LAT, rows), BF16),
                pltpu.VMEM((LAT, rows), BF16),
                pltpu.VMEM((DH, LAT), F32),
                pltpu.VMEM((nx, 4, 128), F32),
                pltpu.VMEM((NZ, 4, 128), F32),
            ]
            + reduce_buffers(8, 8)
            + reduce_buffers(8, 4)
            + [pltpu.SemaphoreType.DMA((len(args),))]
            + [pltpu.SemaphoreType.DMA((1,))] * 22,
            compiler_params=pltpu.CompilerParams(
                collective_id=0, has_side_effects=True, vmem_limit_bytes=48 * 2**20
            ),
            name="perceiver_backward",
        )(*args)
        return pl.pallas_call(
            write_out,
            out_shape=outs,
            in_specs=[vmem] * len(outs),
            out_specs=(hbm,) * len(outs),
            scratch_shapes=[pltpu.SemaphoreType.DMA((len(outs),))],
            compiler_params=pltpu.CompilerParams(vmem_limit_bytes=2**20),
            name="write_out",
        )(*[pltpu.with_memory_space_constraint(x, pltpu.VMEM) for x in made])

    return jax.shard_map(
        on_device,
        mesh=mesh,
        in_specs=(
            P(None, "head"),
            P("seq", "head"),
            P("seq", "head"),
            P(None, "head"),
            P("seq", "head"),
            P(None, "head"),
            P(None, "head"),
            P("seq", "head"),
            P(("seq", "head")),
        ),
        out_specs=(
            P(None, "head"),
            P("seq", "head"),
            P("seq", "head"),
            P("seq", "head"),
            P(None, "head"),
            P(None, "head"),
        ),
        check_vma=False,
    )
```

```python
import functools
import math

import jax
import jax.numpy as jnp
from jax import lax
from jax.experimental import pallas as pl
from jax.experimental.pallas import tpu as pltpu
from jax.sharding import PartitionSpec as P

DH = 128
LAT = 256
NZ = 16
MESH = pl.DeviceIdType.MESH
F32 = jnp.float32
BF16 = jnp.bfloat16
NT = (((1,), (1,)), ((), ()))
NN = (((1,), (0,)), ((), ()))
TN = (((0,), (0,)), ((), ()))


def dot(a, b, dims):
    return lax.dot_general(a, b, dims, preferred_element_type=F32)


def merge_stats(ref, count):
    lses = [ref[i, 0:2, :] for i in range(count)]
    top = functools.reduce(jnp.maximum, lses)
    weights = [jnp.exp(lse - top) for lse in lses]
    total = functools.reduce(jnp.add, weights)
    mixed = functools.reduce(jnp.add, [w * ref[i, 2:4, :] for i, w in enumerate(weights)])
    return top + jnp.log(total), mixed / total


def fold(line):
    return jnp.concatenate([line[:, :128], line[:, 128:]], axis=0)


def kernel(
    nx, nh, rows,
    lq_hbm, pk_hbm, pv_hbm, eg_hbm, pq_hbm, lk_hbm, lv_hbm, dg_hbm, mask_hbm,
    glq_ref, gpk_ref, gpv_ref, gpq_ref, glk_ref, glv_ref,
    lq_ref, pk_ref, pv_ref, eg_ref, pq_ref, lk_ref, lv_ref, dg_ref, mask_ref,
    maskbuf, mcol, expo, edot, esums, dprob, dscore, query_t,
    sx, sz, pdec, rxdec, sumdec, rzdec, fulldec, pq, rxq, sumq, rzq, fullq,
    in_sems,
    m_send, m_recv, sx_send, sx_recv, sz_send, sz_recv,
    dx_send, dx_recv, dz_send, dz_recv, daz_send, daz_recv, dax_send, dax_recv,
    qx_send, qx_recv, qz_send, qz_recv, qaz_send, qaz_recv, qax_send, qax_recv,
):
    scale = 1.0 / math.sqrt(DH)
    piece = rows // nh
    size = 384
    spans = [slice(at, at + size) for at in range(0, rows, size)]
    seq = lax.axis_index("seq")
    head = lax.axis_index("head")
    xi = seq // NZ
    zi = lax.rem(seq, NZ)

    loads = [
        pltpu.make_async_copy(src, dst, in_sems.at[i])
        for i, (src, dst) in enumerate(
            (
                (mask_hbm, mask_ref),
                (pq_hbm, pq_ref),
                (lk_hbm, lk_ref),
                (dg_hbm, dg_ref),
                (lv_hbm, lv_ref),
                (pk_hbm, pk_ref),
                (lq_hbm, lq_ref),
                (pv_hbm, pv_ref),
                (eg_hbm, eg_ref),
            )
        )
    ]
    for load in loads:
        load.start()

    def head_peer(step):
        return lax.rem(head + step, nh)

    def x_peer(step):
        return lax.rem(xi + step, nx)

    def z_peer(step):
        return lax.rem(zi + NZ // 2 + (step // 2) * (2 * lax.rem(step, 2) - 1), NZ)

    def at_head(peer):
        return (seq, peer)

    def at_x(peer):
        return (peer * NZ + zi, head)

    def at_z(peer):
        return (xi * NZ + peer, head)

    def every(count, body):
        def step(i, carry):
            body(i)
            return carry

        lax.fori_loop(1, count, step, 0)

    def send(src, dst, send_sem, recv_sem, target):
        return pltpu.make_async_remote_copy(
            src_ref=src, dst_ref=dst, send_sem=send_sem.at[0], recv_sem=recv_sem.at[0],
            device_id=target, device_id_type=MESH,
        )

    def all_of(ref, count, send_sem, recv_sem, target):
        part = ref.at[pl.ds(0, count - 1)]
        return send(part, part, send_sem, recv_sem, target)

    barrier = pltpu.get_barrier_semaphore()

    def greet(peer_of, place):
        def body(step):
            pl.semaphore_signal(
                barrier, inc=1, device_id=place(peer_of(step)), device_id_type=MESH
            )
        return body

    every(nh, greet(head_peer, at_head))
    every(nx, greet(x_peer, at_x))
    every(NZ, greet(z_peer, at_z))
    loads[0].wait()
    maskbuf[head] = jnp.zeros((1, 384), F32)
    maskbuf[head, :, 0:piece] = (mask_ref[...] > 0).astype(F32).reshape(1, piece)
    pl.semaphore_wait(barrier, nh + nx + NZ - 3)

    every(nh, lambda i: send(
        maskbuf.at[head], maskbuf.at[head], m_send, m_recv, at_head(head_peer(i))
    ).start())

    for load in loads[1:5]:
        load.wait()
    lat_key = lk_ref[...]
    lat_value = lv_ref[...]
    for span in spans:
        score = dot(lat_key, pq_ref[span, :], NT) * scale
        e = jnp.exp(score - jnp.max(score, axis=0, keepdims=True))
        p = e * (1.0 / jnp.sum(e, axis=0, keepdims=True))
        dg = dot(lat_value, dg_ref[span, :], NT)
        dd = jnp.sum(p * dg, axis=0, keepdims=True)
        dprob[:, span] = p.astype(BF16)
        dscore[:, span] = (p * (dg - dd)).astype(BF16)

    for load in loads[5:]:
        load.wait()
    enc_grad = eg_ref[...]
    for span in spans:
        edot[span, :] = dot(pv_ref[span, :], enc_grad, NT)

    mask_all = all_of(maskbuf, nh, m_send, m_recv, at_head(head_peer(1)))
    mask_all.wait_recv()
    for h in range(nh):
        line = jnp.broadcast_to(maskbuf[h], (128, 384))
        mcol[h * piece:(h + 1) * piece, :] = line.T[:piece, :]

    class Sum:
        def __init__(self, part, rx, summed, rz, full, *sems):
            self.part, self.rx, self.summed, self.rz, self.full = part, rx, summed, rz, full
            self.x_sems, self.z_sems = sems[0:2], sems[2:4]
            self.az_sems, self.ax_sems = sems[4:6], sems[6:8]
            self.whole = [
                all_of(rx, nx, *self.x_sems, at_x(x_peer(1))),
                all_of(rz, NZ, *self.z_sems, at_z(z_peer(1))),
                all_of(full.at[xi], NZ, *self.az_sems, at_z(z_peer(1))),
                all_of(full, nx, *self.ax_sems, at_x(x_peer(1))),
            ]

        def scatter_x(self):
            every(nx, lambda i: send(
                self.part.at[x_peer(i)], self.rx.at[xi], *self.x_sems, at_x(x_peer(i))
            ).start())

        def gathered_x(self):
            self.rx[xi] = self.part[xi]
            self.whole[0].wait_recv()

        def scatter_z(self):
            every(NZ, lambda i: send(
                self.summed.at[z_peer(i)], self.rz.at[zi], *self.z_sems, at_z(z_peer(i))
            ).start())

        def gather_z(self):
            self.rz[zi] = self.summed[zi]
            self.whole[1].wait_recv()
            pieces = [self.rz[i] for i in range(NZ)]
            while len(pieces) > 1:
                pieces = [a + b for a, b in zip(pieces[0::2], pieces[1::2])]
            self.full[xi, zi] = pieces[0]
            every(NZ, lambda i: send(
                self.full.at[xi, zi], self.full.at[xi, zi], *self.az_sems, at_z(z_peer(i))
            ).start())

        def gather_x(self):
            self.whole[2].wait_recv()
            every(nx, lambda i: send(
                self.full.at[xi], self.full.at[xi], *self.ax_sems, at_x(x_peer(i))
            ).start())

        def finish(self):
            self.whole[3].wait_recv()

        def drain(self):
            for copy in self.whole:
                copy.wait_send()

    dec = Sum(
        pdec, rxdec, sumdec, rzdec, fulldec,
        dx_send, dx_recv, dz_send, dz_recv, daz_send, daz_recv, dax_send, dax_recv,
    )
    enc = Sum(
        pq, rxq, sumq, rzq, fullq,
        qx_send, qx_recv, qz_send, qz_recv, qaz_send, qaz_recv, qax_send, qax_recv,
    )
    lat_query = lq_ref[...]
    tops, totals, deltas = [], [], []
    for span in spans:
        bias = (mcol[span, :] - 1.0) * 1e30
        score = dot(pk_ref[span, :], lat_query, NT) * scale
        score = score + jnp.concatenate([bias, bias], axis=1)
        grad = edot[span, :]
        own = jnp.max(score, axis=0, keepdims=True)
        e = jnp.exp(score - own)
        expo[span, :] = e
        own_total = jnp.sum(e, axis=0, keepdims=True)
        own_delta = jnp.sum(e * grad, axis=0, keepdims=True) / own_total
        esums[span, :LAT] = (e * (grad - own_delta)).astype(BF16)
        esums[span, LAT:] = e.astype(BF16)
        tops.append(own)
        totals.append(own_total)
        deltas.append(own_delta)
    top = functools.reduce(jnp.maximum, tops)
    shares = [jnp.exp(own - top) for own in tops]
    weights = [w * t for w, t in zip(shares, totals)]
    total = functools.reduce(jnp.add, weights)
    inverse = 1.0 / total
    delta = functools.reduce(jnp.add, [w * d for w, d in zip(weights, deltas)]) * inverse

    def put_stats(ref, slot, lse_rows, delta_rows):
        ref[slot, 0:2, :] = lse_rows
        ref[slot, 2:4, :] = delta_rows

    put_stats(sx, xi, fold(top + jnp.log(total)), fold(delta))
    every(nx, lambda i: send(sx.at[xi], sx.at[xi], sx_send, sx_recv, at_x(x_peer(i))).start())

    a = jnp.zeros((DH, LAT), F32)
    b = jnp.zeros((DH, LAT), F32)
    for span, w, d in zip(spans, shares, deltas):
        sums = dot(pk_ref[span, :], esums[span, :], TN)
        w = w * inverse
        a = a + w * (sums[:, :LAT] + (d - delta) * sums[:, LAT:])
        b = b + w * sums[:, LAT:]

    def place(i, j):
        at = i * (DH // nx) + (j // 2) * 4
        return slice(at, at + 4), slice((j % 2) * 128, (j % 2) * 128 + 128)

    for i in range(nx):
        for j in range(NZ):
            pq[i, j] = jnp.concatenate([a[place(i, j)], b[place(i, j)]], axis=0)
    enc.scatter_x()

    key_sum = jnp.zeros((LAT, DH), F32)
    value_sum = jnp.zeros((LAT, DH), F32)
    for span in spans:
        valid = mcol[span, :].astype(BF16)
        key_sum = key_sum + dot(dscore[:, span], pq_ref[span, :] * valid, NN)
        value_sum = value_sum + dot(dprob[:, span], dg_ref[span, :] * valid, NN)
    pdec[0:nx // 2] = key_sum.reshape(nx // 2, NZ, 8, 128)
    pdec[nx // 2:nx] = value_sum.reshape(nx // 2, NZ, 8, 128)
    dec.scatter_x()

    sx_all = all_of(sx, nx, sx_send, sx_recv, at_x(x_peer(1)))
    sx_all.wait_recv()
    put_stats(sz, zi, *merge_stats(sx, nx))
    every(NZ, lambda i: send(sz.at[zi], sz.at[zi], sz_send, sz_recv, at_z(z_peer(i))).start())

    for span in spans:
        grad = dot(dscore[:, span], lat_key, TN) * (mcol[span, :] * scale)
        gpq_ref[span, :] = grad.astype(BF16)

    dec.gathered_x()
    sumdec[...] = (rxdec[0] + rxdec[1]) + (rxdec[2] + rxdec[3])
    dec.scatter_z()

    sz_all = all_of(sz, NZ, sz_send, sz_recv, at_z(z_peer(1)))
    sz_all.wait_recv()
    lse2, delta2 = merge_stats(sz, NZ)
    enc.gathered_x()
    factors = [jnp.exp(sx[i, 0:2, :] - lse2) for i in range(nx)]
    shifts = [sx[i, 2:4, :] - delta2 for i in range(nx)]
    for j in range(NZ):
        half = slice(j % 2, j % 2 + 1)
        terms = [
            factors[i][half] * (rxq[i, j, 0:4, :] + shifts[i][half] * rxq[i, j, 4:8, :])
            for i in range(nx)
        ]
        sumq[j] = functools.reduce(jnp.add, terms)
    enc.scatter_z()

    lse = jnp.concatenate([lse2[0:1], lse2[1:2]], axis=1)
    delta = jnp.concatenate([delta2[0:1], delta2[1:2]], axis=1)

    def enc_packets(first, last):
        for span, own in zip(spans[first:last], tops[first:last]):
            p = expo[span, :] * jnp.exp(own - lse)
            ds = (p * (edot[span, :] - delta)).astype(BF16)
            gpk_ref[span, :] = (dot(ds, lat_query, NN) * scale).astype(BF16)
            gpv_ref[span, :] = dot(p.astype(BF16), enc_grad, NN).astype(BF16)

    enc_packets(0, 3)
    dec.gather_z()
    enc_packets(3, len(spans))
    enc.gather_z()
    dec.gather_x()
    enc.gather_x()
    dec.finish()
    glk_ref[...] = (fulldec[0:nx // 2].reshape(LAT, DH) * scale).astype(BF16)
    glv_ref[...] = fulldec[nx // 2:nx].reshape(LAT, DH)
    enc.finish()
    for i in range(nx):
        for k in range(0, NZ, 4):
            for c in range(2):
                at, lanes = place(i, k + c)
                query_t[at.start:at.start + 8, lanes] = jnp.concatenate(
                    [fullq[i, k + c], fullq[i, k + 2 + c]], axis=0
                )
    glq_ref[...] = (query_t[...].T * scale).astype(BF16)

    mask_all.wait_send()
    sx_all.wait_send()
    sz_all.wait_send()
    dec.drain()
    enc.drain()


def write_out(*refs):
    count = len(refs) // 2
    sems = refs[-1]
    copies = [
        pltpu.make_async_copy(refs[i], refs[count + i], sems.at[i]) for i in range(count)
    ]
    for copy in copies:
        copy.start()
    for copy in copies:
        copy.wait()


def solution(mesh):
    nx = mesh.shape["seq"] // NZ
    nh = mesh.shape["head"]

    def on_device(lq, pk, pv, eg, pq, lk, lv, dg, mask):
        rows = pk.shape[0]
        vmem = pl.BlockSpec(memory_space=pltpu.VMEM)
        hbm = pl.BlockSpec(memory_space=pltpu.HBM)
        lat = jax.ShapeDtypeStruct((LAT, DH), BF16)
        pkt = jax.ShapeDtypeStruct((rows, DH), BF16)
        outs = (lat, pkt, pkt, pkt, lat, jax.ShapeDtypeStruct((LAT, DH), F32))
        args = [
            pltpu.with_memory_space_constraint(x, pltpu.HBM)
            for x in (lq, pk, pv, eg, pq, lk, lv, dg, mask)
        ]

        def reduce_buffers(sent, depth):
            return [
                pltpu.VMEM((nx, NZ, sent, 128), F32),
                pltpu.VMEM((nx, NZ, sent, 128), F32),
                pltpu.VMEM((NZ, depth, 128), F32),
                pltpu.VMEM((NZ, depth, 128), F32),
                pltpu.VMEM((nx, NZ, depth, 128), F32),
            ]

        made = pl.pallas_call(
            functools.partial(kernel, nx, nh, rows),
            out_shape=outs,
            in_specs=[hbm] * len(args),
            out_specs=(vmem,) * len(outs),
            scratch_shapes=[pltpu.VMEM(x.shape, x.dtype) for x in args]
            + [
                pltpu.VMEM((nh, 1, 384), F32),
                pltpu.VMEM((rows, 128), F32),
                pltpu.VMEM((rows, LAT), F32),
                pltpu.VMEM((rows, LAT), F32),
                pltpu.VMEM((rows, 2 * LAT), BF16),
                pltpu.VMEM((LAT, rows), BF16),
                pltpu.VMEM((LAT, rows), BF16),
                pltpu.VMEM((DH, LAT), F32),
                pltpu.VMEM((nx, 4, 128), F32),
                pltpu.VMEM((NZ, 4, 128), F32),
            ]
            + reduce_buffers(8, 8)
            + reduce_buffers(8, 4)
            + [pltpu.SemaphoreType.DMA((len(args),))]
            + [pltpu.SemaphoreType.DMA((1,))] * 22,
            compiler_params=pltpu.CompilerParams(
                collective_id=0, has_side_effects=True, vmem_limit_bytes=48 * 2**20
            ),
            name="perceiver_backward",
        )(*args)
        return pl.pallas_call(
            write_out,
            out_shape=outs,
            in_specs=[vmem] * len(outs),
            out_specs=(hbm,) * len(outs),
            scratch_shapes=[pltpu.SemaphoreType.DMA((len(outs),))],
            compiler_params=pltpu.CompilerParams(vmem_limit_bytes=2**20),
            name="write_out",
        )(*[pltpu.with_memory_space_constraint(x, pltpu.VMEM) for x in made])

    return jax.shard_map(
        on_device,
        mesh=mesh,
        in_specs=(
            P(None, "head"),
            P("seq", "head"),
            P("seq", "head"),
            P(None, "head"),
            P("seq", "head"),
            P(None, "head"),
            P(None, "head"),
            P("seq", "head"),
            P(("seq", "head")),
        ),
        out_specs=(
            P(None, "head"),
            P("seq", "head"),
            P("seq", "head"),
            P("seq", "head"),
            P(None, "head"),
            P(None, "head"),
        ),
        check_vma=False,
    )
```

```python
import functools
import math

import jax
import jax.numpy as jnp
from jax import lax
from jax.experimental import pallas as pl
from jax.experimental.pallas import tpu as pltpu
from jax.sharding import PartitionSpec as P

DH = 128
LAT = 256
NZ = 16
MESH = pl.DeviceIdType.MESH
F32 = jnp.float32
BF16 = jnp.bfloat16
NT = (((1,), (1,)), ((), ()))
NN = (((1,), (0,)), ((), ()))
TN = (((0,), (0,)), ((), ()))


def dot(a, b, dims):
    return lax.dot_general(a, b, dims, preferred_element_type=F32)


def merge_stats(ref, count):
    lses = [ref[i, 0:2, :] for i in range(count)]
    top = functools.reduce(jnp.maximum, lses)
    weights = [jnp.exp(lse - top) for lse in lses]
    total = functools.reduce(jnp.add, weights)
    mixed = functools.reduce(jnp.add, [w * ref[i, 2:4, :] for i, w in enumerate(weights)])
    return top + jnp.log(total), mixed / total


def fold(line):
    return jnp.concatenate([line[:, :128], line[:, 128:]], axis=0)


def kernel(
    nx, nh, rows,
    lq_hbm, pk_hbm, pv_hbm, eg_hbm, pq_hbm, lk_hbm, lv_hbm, dg_hbm, mask_hbm,
    glq_ref, gpk_ref, gpv_ref, gpq_ref, glk_ref, glv_ref,
    lq_ref, pk_ref, pv_ref, eg_ref, pq_ref, lk_ref, lv_ref, dg_ref, mask_ref,
    maskbuf, mcol, expo, edot, esums, dprob, dscore, query_t,
    sx, sz, pdec, rxdec, sumdec, rzdec, fulldec, pq, rxq, sumq, rzq, fullq,
    in_sems,
    m_send, m_recv, sx_send, sx_recv, sz_send, sz_recv,
    dx_send, dx_recv, dz_send, dz_recv, daz_send, daz_recv, dax_send, dax_recv,
    qx_send, qx_recv, qz_send, qz_recv, qaz_send, qaz_recv, qax_send, qax_recv,
):
    scale = 1.0 / math.sqrt(DH)
    piece = rows // nh
    size = 384
    spans = [slice(at, at + size) for at in range(0, rows, size)]
    seq = lax.axis_index("seq")
    head = lax.axis_index("head")
    xi = seq // NZ
    zi = lax.rem(seq, NZ)

    loads = [
        pltpu.make_async_copy(src, dst, in_sems.at[i])
        for i, (src, dst) in enumerate(
            (
                (mask_hbm, mask_ref),
                (pq_hbm, pq_ref),
                (lk_hbm, lk_ref),
                (dg_hbm, dg_ref),
                (lv_hbm, lv_ref),
                (pk_hbm, pk_ref),
                (lq_hbm, lq_ref),
                (pv_hbm, pv_ref),
                (eg_hbm, eg_ref),
            )
        )
    ]
    for load in loads:
        load.start()

    def head_peer(step):
        return lax.rem(head + step, nh)

    def x_peer(step):
        return lax.rem(xi + step, nx)

    def z_peer(step):
        return lax.rem(zi + NZ // 2 + (step // 2) * (2 * lax.rem(step, 2) - 1), NZ)

    def at_head(peer):
        return (seq, peer)

    def at_x(peer):
        return (peer * NZ + zi, head)

    def at_z(peer):
        return (xi * NZ + peer, head)

    def every(count, body):
        def step(i, carry):
            body(i)
            return carry

        lax.fori_loop(1, count, step, 0, unroll=True)

    def send(src, dst, send_sem, recv_sem, target):
        return pltpu.make_async_remote_copy(
            src_ref=src, dst_ref=dst, send_sem=send_sem.at[0], recv_sem=recv_sem.at[0],
            device_id=target, device_id_type=MESH,
        )

    def all_of(ref, count, send_sem, recv_sem, target):
        part = ref.at[pl.ds(0, count - 1)]
        return send(part, part, send_sem, recv_sem, target)

    barrier = pltpu.get_barrier_semaphore()

    def greet(peer_of, place):
        def body(step):
            pl.semaphore_signal(
                barrier, inc=1, device_id=place(peer_of(step)), device_id_type=MESH
            )
        return body

    every(nh, greet(head_peer, at_head))
    every(nx, greet(x_peer, at_x))
    every(NZ, greet(z_peer, at_z))
    loads[0].wait()
    maskbuf[head] = jnp.zeros((1, 384), F32)
    maskbuf[head, :, 0:piece] = (mask_ref[...] > 0).astype(F32).reshape(1, piece)
    pl.semaphore_wait(barrier, nh + nx + NZ - 3)

    every(nh, lambda i: send(
        maskbuf.at[head], maskbuf.at[head], m_send, m_recv, at_head(head_peer(i))
    ).start())

    for load in loads[1:5]:
        load.wait()
    lat_key = lk_ref[...]
    lat_value = lv_ref[...]
    for span in spans:
        score = dot(lat_key, pq_ref[span, :], NT) * scale
        e = jnp.exp(score - jnp.max(score, axis=0, keepdims=True))
        p = e * (1.0 / jnp.sum(e, axis=0, keepdims=True))
        dg = dot(lat_value, dg_ref[span, :], NT)
        dd = jnp.sum(p * dg, axis=0, keepdims=True)
        dprob[:, span] = p.astype(BF16)
        dscore[:, span] = (p * (dg - dd)).astype(BF16)

    mask_all = all_of(maskbuf, nh, m_send, m_recv, at_head(head_peer(1)))
    mask_all.wait_recv()
    for h in range(nh):
        line = jnp.broadcast_to(maskbuf[h], (128, 384))
        mcol[h * piece:(h + 1) * piece, :] = line.T[:piece, :]

    class Sum:
        def __init__(self, part, rx, summed, rz, full, *sems):
            self.part, self.rx, self.summed, self.rz, self.full = part, rx, summed, rz, full
            self.x_sems, self.z_sems = sems[0:2], sems[2:4]
            self.az_sems, self.ax_sems = sems[4:6], sems[6:8]
            self.whole = [
                all_of(rx, nx, *self.x_sems, at_x(x_peer(1))),
                all_of(rz, NZ, *self.z_sems, at_z(z_peer(1))),
                all_of(full.at[xi], NZ, *self.az_sems, at_z(z_peer(1))),
                all_of(full, nx, *self.ax_sems, at_x(x_peer(1))),
            ]

        def scatter_x(self):
            every(nx, lambda i: send(
                self.part.at[x_peer(i)], self.rx.at[xi], *self.x_sems, at_x(x_peer(i))
            ).start())

        def gathered_x(self):
            self.rx[xi] = self.part[xi]
            self.whole[0].wait_recv()

        def scatter_z(self):
            every(NZ, lambda i: send(
                self.summed.at[z_peer(i)], self.rz.at[zi], *self.z_sems, at_z(z_peer(i))
            ).start())

        def gather_z(self):
            self.rz[zi] = self.summed[zi]
            self.whole[1].wait_recv()
            pieces = [self.rz[i] for i in range(NZ)]
            while len(pieces) > 1:
                pieces = [a + b for a, b in zip(pieces[0::2], pieces[1::2])]
            self.full[xi, zi] = pieces[0]
            every(NZ, lambda i: send(
                self.full.at[xi, zi], self.full.at[xi, zi], *self.az_sems, at_z(z_peer(i))
            ).start())

        def gather_x(self):
            self.whole[2].wait_recv()
            every(nx, lambda i: send(
                self.full.at[xi], self.full.at[xi], *self.ax_sems, at_x(x_peer(i))
            ).start())

        def finish(self):
            self.whole[3].wait_recv()

        def drain(self):
            for copy in self.whole:
                copy.wait_send()

    dec = Sum(
        pdec, rxdec, sumdec, rzdec, fulldec,
        dx_send, dx_recv, dz_send, dz_recv, daz_send, daz_recv, dax_send, dax_recv,
    )
    enc = Sum(
        pq, rxq, sumq, rzq, fullq,
        qx_send, qx_recv, qz_send, qz_recv, qaz_send, qaz_recv, qax_send, qax_recv,
    )
    for load in loads[5:]:
        load.wait()
    lat_query = lq_ref[...]
    enc_grad = eg_ref[...]
    tops, totals, deltas = [], [], []
    for span in spans:
        bias = (mcol[span, :] - 1.0) * 1e30
        score = dot(pk_ref[span, :], lat_query, NT) * scale
        score = score + jnp.concatenate([bias, bias], axis=1)
        grad = dot(pv_ref[span, :], enc_grad, NT)
        own = jnp.max(score, axis=0, keepdims=True)
        e = jnp.exp(score - own)
        expo[span, :] = e
        edot[span, :] = grad
        own_total = jnp.sum(e, axis=0, keepdims=True)
        own_delta = jnp.sum(e * grad, axis=0, keepdims=True) / own_total
        esums[span, :LAT] = (e * (grad - own_delta)).astype(BF16)
        esums[span, LAT:] = e.astype(BF16)
        tops.append(own)
        totals.append(own_total)
        deltas.append(own_delta)
    top = functools.reduce(jnp.maximum, tops)
    shares = [jnp.exp(own - top) for own in tops]
    weights = [w * t for w, t in zip(shares, totals)]
    total = functools.reduce(jnp.add, weights)
    inverse = 1.0 / total
    delta = functools.reduce(jnp.add, [w * d for w, d in zip(weights, deltas)]) * inverse

    def put_stats(ref, slot, lse_rows, delta_rows):
        ref[slot, 0:2, :] = lse_rows
        ref[slot, 2:4, :] = delta_rows

    put_stats(sx, xi, fold(top + jnp.log(total)), fold(delta))
    every(nx, lambda i: send(sx.at[xi], sx.at[xi], sx_send, sx_recv, at_x(x_peer(i))).start())

    key_sum = jnp.zeros((LAT, DH), F32)
    value_sum = jnp.zeros((LAT, DH), F32)
    for span in spans:
        valid = mcol[span, :].astype(BF16)
        key_sum = key_sum + dot(dscore[:, span], pq_ref[span, :] * valid, NN)
        value_sum = value_sum + dot(dprob[:, span], dg_ref[span, :] * valid, NN)
    pdec[0:nx // 2] = key_sum.reshape(nx // 2, NZ, 8, 128)
    pdec[nx // 2:nx] = value_sum.reshape(nx // 2, NZ, 8, 128)
    dec.scatter_x()

    sx_all = all_of(sx, nx, sx_send, sx_recv, at_x(x_peer(1)))
    sx_all.wait_recv()
    put_stats(sz, zi, *merge_stats(sx, nx))
    every(NZ, lambda i: send(sz.at[zi], sz.at[zi], sz_send, sz_recv, at_z(z_peer(i))).start())

    a = jnp.zeros((DH, LAT), F32)
    b = jnp.zeros((DH, LAT), F32)
    for span, w, d in zip(spans, shares, deltas):
        sums = dot(pk_ref[span, :], esums[span, :], TN)
        w = w * inverse
        a = a + w * (sums[:, :LAT] + (d - delta) * sums[:, LAT:])
        b = b + w * sums[:, LAT:]

    def place(i, j):
        at = i * (DH // nx) + (j // 2) * 4
        return slice(at, at + 4), slice((j % 2) * 128, (j % 2) * 128 + 128)

    for i in range(nx):
        for j in range(NZ):
            pq[i, j] = jnp.concatenate([a[place(i, j)], b[place(i, j)]], axis=0)
    enc.scatter_x()

    for span in spans:
        grad = dot(dscore[:, span], lat_key, TN) * (mcol[span, :] * scale)
        gpq_ref[span, :] = grad.astype(BF16)

    dec.gathered_x()
    sumdec[...] = (rxdec[0] + rxdec[1]) + (rxdec[2] + rxdec[3])
    dec.scatter_z()

    sz_all = all_of(sz, NZ, sz_send, sz_recv, at_z(z_peer(1)))
    sz_all.wait_recv()
    lse2, delta2 = merge_stats(sz, NZ)
    enc.gathered_x()
    factors = [jnp.exp(sx[i, 0:2, :] - lse2) for i in range(nx)]
    shifts = [sx[i, 2:4, :] - delta2 for i in range(nx)]
    for j in range(NZ):
        half = slice(j % 2, j % 2 + 1)
        terms = [
            factors[i][half] * (rxq[i, j, 0:4, :] + shifts[i][half] * rxq[i, j, 4:8, :])
            for i in range(nx)
        ]
        sumq[j] = functools.reduce(jnp.add, terms)
    enc.scatter_z()

    lse = jnp.concatenate([lse2[0:1], lse2[1:2]], axis=1)
    delta = jnp.concatenate([delta2[0:1], delta2[1:2]], axis=1)

    def enc_packets(first, last):
        for span, own in zip(spans[first:last], tops[first:last]):
            p = expo[span, :] * jnp.exp(own - lse)
            ds = (p * (edot[span, :] - delta)).astype(BF16)
            gpk_ref[span, :] = (dot(ds, lat_query, NN) * scale).astype(BF16)
            gpv_ref[span, :] = dot(p.astype(BF16), enc_grad, NN).astype(BF16)

    enc_packets(0, 3)
    dec.gather_z()
    enc_packets(3, len(spans))
    enc.gather_z()
    dec.gather_x()
    enc.gather_x()
    dec.finish()
    glk_ref[...] = (fulldec[0:nx // 2].reshape(LAT, DH) * scale).astype(BF16)
    glv_ref[...] = fulldec[nx // 2:nx].reshape(LAT, DH)
    enc.finish()
    for i in range(nx):
        for k in range(0, NZ, 4):
            for c in range(2):
                at, lanes = place(i, k + c)
                query_t[at.start:at.start + 8, lanes] = jnp.concatenate(
                    [fullq[i, k + c], fullq[i, k + 2 + c]], axis=0
                )
    glq_ref[...] = (query_t[...].T * scale).astype(BF16)

    mask_all.wait_send()
    sx_all.wait_send()
    sz_all.wait_send()
    dec.drain()
    enc.drain()


def write_out(*refs):
    count = len(refs) // 2
    sems = refs[-1]
    copies = [
        pltpu.make_async_copy(refs[i], refs[count + i], sems.at[i]) for i in range(count)
    ]
    for copy in copies:
        copy.start()
    for copy in copies:
        copy.wait()


def solution(mesh):
    nx = mesh.shape["seq"] // NZ
    nh = mesh.shape["head"]

    def on_device(lq, pk, pv, eg, pq, lk, lv, dg, mask):
        rows = pk.shape[0]
        vmem = pl.BlockSpec(memory_space=pltpu.VMEM)
        hbm = pl.BlockSpec(memory_space=pltpu.HBM)
        lat = jax.ShapeDtypeStruct((LAT, DH), BF16)
        pkt = jax.ShapeDtypeStruct((rows, DH), BF16)
        outs = (lat, pkt, pkt, pkt, lat, jax.ShapeDtypeStruct((LAT, DH), F32))
        args = [
            pltpu.with_memory_space_constraint(x, pltpu.HBM)
            for x in (lq, pk, pv, eg, pq, lk, lv, dg, mask)
        ]

        def reduce_buffers(sent, depth):
            return [
                pltpu.VMEM((nx, NZ, sent, 128), F32),
                pltpu.VMEM((nx, NZ, sent, 128), F32),
                pltpu.VMEM((NZ, depth, 128), F32),
                pltpu.VMEM((NZ, depth, 128), F32),
                pltpu.VMEM((nx, NZ, depth, 128), F32),
            ]

        made = pl.pallas_call(
            functools.partial(kernel, nx, nh, rows),
            out_shape=outs,
            in_specs=[hbm] * len(args),
            out_specs=(vmem,) * len(outs),
            scratch_shapes=[pltpu.VMEM(x.shape, x.dtype) for x in args]
            + [
                pltpu.VMEM((nh, 1, 384), F32),
                pltpu.VMEM((rows, 128), F32),
                pltpu.VMEM((rows, LAT), F32),
                pltpu.VMEM((rows, LAT), F32),
                pltpu.VMEM((rows, 2 * LAT), BF16),
                pltpu.VMEM((LAT, rows), BF16),
                pltpu.VMEM((LAT, rows), BF16),
                pltpu.VMEM((DH, LAT), F32),
                pltpu.VMEM((nx, 4, 128), F32),
                pltpu.VMEM((NZ, 4, 128), F32),
            ]
            + reduce_buffers(8, 8)
            + reduce_buffers(8, 4)
            + [pltpu.SemaphoreType.DMA((len(args),))]
            + [pltpu.SemaphoreType.DMA((1,))] * 22,
            compiler_params=pltpu.CompilerParams(
                collective_id=0, has_side_effects=True, vmem_limit_bytes=48 * 2**20
            ),
            name="perceiver_backward",
        )(*args)
        return pl.pallas_call(
            write_out,
            out_shape=outs,
            in_specs=[vmem] * len(outs),
            out_specs=(hbm,) * len(outs),
            scratch_shapes=[pltpu.SemaphoreType.DMA((len(outs),))],
            compiler_params=pltpu.CompilerParams(vmem_limit_bytes=2**20),
            name="write_out",
        )(*[pltpu.with_memory_space_constraint(x, pltpu.VMEM) for x in made])

    return jax.shard_map(
        on_device,
        mesh=mesh,
        in_specs=(
            P(None, "head"),
            P("seq", "head"),
            P("seq", "head"),
            P(None, "head"),
            P("seq", "head"),
            P(None, "head"),
            P(None, "head"),
            P("seq", "head"),
            P(("seq", "head")),
        ),
        out_specs=(
            P(None, "head"),
            P("seq", "head"),
            P("seq", "head"),
            P("seq", "head"),
            P(None, "head"),
            P(None, "head"),
        ),
        check_vma=False,
    )
```
